32 devices in a mesh: groups: 2 (over y), fsdp: 8 (over z, x), blk: 2 (over core).
Axes of the slice: x: 2, y: 2, z: 4, core: 2. Of those that a mesh axis runs over, the one named last changes fastest.
Arguments:
- block_input: bfloat16 [8192, 5120], P(('groups', 'fsdp', 'blk')), parts along dimension 0, may hold values from -3 to 3
- gate: float32 [10240], P('groups'), parts along dimension 0, may hold values from -6 to 6
- q_fresh: bfloat16 [8192, 2560], P(('groups', 'fsdp', 'blk')), parts along dimension 0, may hold values from -48.5 to 48.5
- kv_fresh: bfloat16 [8192, 2, 2560], P(('groups', 'fsdp', 'blk')), parts along dimension 0, may hold values from -6 to 6
- kv_cache: bfloat16 [8192, 2, 2560], P(('groups', 'fsdp', 'blk')), parts along dimension 0, may hold values from -6 to 6
- active_list: int32 [16, 2, 2], P(('groups', 'fsdp')), parts along dimension 0, may hold values from 0 to 1, as said below
- active_count: int32 [16, 2], P(('groups', 'fsdp')), parts along dimension 0, may hold values from 0 to 2, as said below
- key_list: int32 [16, 4, 3], P(('groups', 'fsdp')), parts along dimension 0, may hold values from 0 to 3, as said below
- out_weight: bfloat16 [2560, 5120], P('fsdp'), may hold values from -0.125 to 0.125
Outputs:
- block_output: bfloat16 [8192, 5120], P(('groups', 'fsdp', 'blk')), parts along dimension 0
The draws below stay inside these ranges and needn't reach their ends.
There are 2 independent parts, one for each index of `groups`. The reference program is written for one: setup_inputs(seed, part) draws one part's arguments, and reference() takes and returns one part's arrays. A program takes and returns all parts, laid end to end along the dimension named above; an argument that names none is the same for every part. Nothing has to cross between parts.
Inputs may be any that keep to these rules, and one draw needn't show every extreme that they name: `active_list`: each row [f, b] holds every tile number once; its first active_count[f, b] entries are the active tiles. `active_count`: some token block has all 2 tiles active. `key_list`: entry [f, g] holds 3 different tile ids of group f, the first one being g.
All inputs are finite; a program needn't handle non-finite values.
Results may differ from the reference program's by a relative error of at most 0.0034.
Values may be sent and summed in bfloat16 or wider, within the bound.
No kernel may reach another device: no remote copies, remote signals or barrier semaphores. Data moves between devices by JAX's collectives and lax.ppermute only.
A program may use at most 128 MiB of HBM per device.

```python
import math
import jax
import jax.numpy as jnp
from jax import lax

D = 5120
HEADS = 20
HEAD_DIM = 128
TILE = 128
TILES_DEV = 2
HD = 2560
TOK_DEV = 256
GROUP_TILES = 4
KEY_TILES = 3
TOKENS = 4096
N_FSDP = 8
N_BLK = 2


def fresh_pair(key):
    base_key = jax.random.fold_in(key, 37)
    query_key, keys_key, values_key = jax.random.split(base_key, 3)
    queries = jnp.clip(2.0 * jax.random.normal(query_key, (TOKENS, HD), jnp.float32), -8.0, 8.0)
    key_rows = jnp.clip(jax.random.normal(keys_key, (TOKENS, HD), jnp.float32), -6.0, 6.0)
    value_rows = jnp.clip(jax.random.normal(values_key, (TOKENS, HD), jnp.float32), -6.0, 6.0)
    return (queries, jnp.stack([key_rows, value_rows], axis=1))


def draw_q_fresh(key, part):
    return fresh_pair(key)[0].astype(jnp.bfloat16)


def draw_kv_fresh(key, part):
    return fresh_pair(key)[1].astype(jnp.bfloat16)


def active_pair(key):
    base_key = jax.random.fold_in(key, 11)
    count_key, pick_key, order_key = jax.random.split(base_key, 3)
    block_count = N_FSDP * N_BLK
    counts = jax.random.randint(count_key, (block_count,), 0, TILES_DEV + 1)
    full_block = jax.random.randint(pick_key, (), 0, block_count)
    counts = jnp.where(jnp.arange(block_count, dtype=jnp.int32) == full_block, TILES_DEV, counts)
    ranking = jax.random.randint(order_key, (block_count, TILES_DEV), 0, 1 << 20) * TILES_DEV + jnp.arange(TILES_DEV, dtype=jnp.int32)[None, :]
    ordering = jnp.argsort(ranking, axis=1, stable=True).astype(jnp.int32)
    return (ordering.reshape(N_FSDP, N_BLK, TILES_DEV), counts.astype(jnp.int32).reshape(N_FSDP, N_BLK))


def draw_active_list(key, part):
    return active_pair(key)[0]


def draw_active_count(key, part):
    return active_pair(key)[1]


def draw_key_list(key, part):
    base_key = jax.random.fold_in(key, 23)
    tile_ids = jnp.arange(GROUP_TILES, dtype=jnp.int32)
    ranking = jax.random.randint(base_key, (N_FSDP, GROUP_TILES, GROUP_TILES), 0, 1 << 20) * GROUP_TILES + tile_ids[None, None, :]
    ranking = jnp.where(tile_ids[None, :, None] == tile_ids[None, None, :], -1, ranking)
    ordering = jnp.argsort(ranking, axis=2, stable=True).astype(jnp.int32)
    return ordering[:, :, :KEY_TILES]


def levels(rng, dims, cuts, low, top_value):
    level, own = 1.0, jax.random.fold_in(rng, 6)
    for dim, shards_of in cuts:
        draws = jnp.exp(jax.random.uniform(jax.random.fold_in(own, dim), (shards_of,), jnp.float32, low / len(cuts), top_value / len(cuts)))
        level = level * jnp.repeat(draws, dims[dim] // shards_of).reshape([-1 if axis == dim else 1 for axis in range(len(dims))])
    return level


def scatter_about(rng, shape, deviation, bound, shards=(), held_as=jnp.bfloat16):
    result = jax.random.normal(rng, shape, jnp.float32) * deviation
    if len(shards) > 0:
        result = levels(rng, shape, shards, -0.22, 0.18) * result
    return jnp.clip(result, min=-bound, max=bound).astype(held_as)


def setup_inputs(seed: int = 0, part: int = 0) -> dict:
    seeds = jax.random.split(jax.random.key(seed), 10)
    own_keys = jax.random.split(jax.random.fold_in(seeds[9], part), 10)
    return {
        "block_input": scatter_about(own_keys[0], (TOKENS, D), 0.5, 3.0, ((0, 16),)),
        "gate": scatter_about(own_keys[1], (D,), 1.5, 6.0, (), jnp.float32),
        "q_fresh": draw_q_fresh(jax.random.fold_in(jax.random.fold_in(seeds[9], part), 71), part),
        "kv_fresh": draw_kv_fresh(jax.random.fold_in(jax.random.fold_in(seeds[9], part), 71), part),
        "kv_cache": scatter_about(own_keys[4], (TOKENS, 2, HD), 1.0, 6.0, ((0, 16),)),
        "active_list": draw_active_list(jax.random.fold_in(jax.random.fold_in(seeds[9], part), 71), part),
        "active_count": draw_active_count(jax.random.fold_in(jax.random.fold_in(seeds[9], part), 71), part),
        "key_list": draw_key_list(jax.random.fold_in(jax.random.fold_in(seeds[9], part), 71), part),
        "out_weight": scatter_about(seeds[8], (HD, D), HD ** -0.5, 0.125, ((0, 8),)),
    }


MASKED = -1e+30

def block_partial(query_tile, key_rows, value_rows, allowed):
    tile_rows = query_tile.shape[0]
    query3 = query_tile.astype(jnp.float32).reshape(tile_rows, HEADS, HEAD_DIM)
    key3 = key_rows.astype(jnp.float32).reshape(key_rows.shape[0], HEADS, HEAD_DIM)
    value3 = value_rows.astype(jnp.float32).reshape(value_rows.shape[0], HEADS, HEAD_DIM)
    scores = jnp.einsum('qhd,khd->hqk', query3, key3) / math.sqrt(HEAD_DIM)
    scores = jnp.where(allowed[None, None, :], scores, MASKED)
    row_max = lax.optimization_barrier(jnp.max(scores, axis=2))
    exp_terms = jnp.where(allowed[None, None, :], jnp.exp(scores - row_max[:, :, None]), 0.0)
    row_total = lax.optimization_barrier(jnp.sum(exp_terms, axis=2))
    weights = lax.optimization_barrier(exp_terms.astype(jnp.bfloat16)).astype(jnp.float32)
    block_out = jnp.einsum('hqk,khd->hqd', weights, value3)
    return (block_out, row_max, row_total)

def reference(block_input, gate, q_fresh, kv_fresh, kv_cache, active_list, active_count, key_list, out_weight):
    block_count = N_FSDP * N_BLK
    slot_ids = jnp.arange(TILES_DEV, dtype=jnp.int32)
    tile_lists = active_list.reshape(block_count, TILES_DEV)
    tile_counts = active_count.reshape(block_count)
    listed = (tile_lists[:, :, None] == slot_ids[None, None, :]) & (slot_ids[None, :, None] < tile_counts[:, None, None])
    tile_active = jnp.any(listed, axis=1).reshape(block_count * TILES_DEV)
    row_active = jnp.repeat(tile_active, TILE)
    resident = jnp.where(row_active[:, None, None], kv_fresh, kv_cache)

    def one_tile(tile_index):
        group_id = tile_index // GROUP_TILES
        group_tile = tile_index % GROUP_TILES
        row_start = tile_index * TILE
        input_tile = lax.dynamic_slice_in_dim(block_input, row_start, TILE, 0)

        def compute_tile():
            query_tile = lax.dynamic_slice_in_dim(q_fresh, row_start, TILE, 0)
            listed_keys = key_list[group_id, group_tile]
            partials = []
            for key_side in range(N_BLK):
                row_base = (group_id * N_BLK + key_side) * TOK_DEV
                block_kv = lax.dynamic_slice_in_dim(resident, row_base, TOK_DEV, 0)
                key_tiles = key_side * TILES_DEV + slot_ids
                allowed_tiles = jnp.any(key_tiles[:, None] == listed_keys[None, :], axis=1)
                allowed = jnp.repeat(allowed_tiles, TILE)
                partials.append(block_partial(query_tile, block_kv[:, 0], block_kv[:, 1], allowed))
            joint_max = jnp.maximum(partials[0][1], partials[1][1])
            scale_zero = jnp.exp(partials[0][1] - joint_max)
            scale_one = jnp.exp(partials[1][1] - joint_max)
            summed = partials[0][0] * scale_zero[:, :, None] + partials[1][0] * scale_one[:, :, None]
            denom = partials[0][2] * scale_zero + partials[1][2] * scale_one
            attended = (summed / denom[:, :, None]).transpose(1, 0, 2).reshape(TILE, HD).astype(jnp.bfloat16)
            projected = jnp.dot(attended, out_weight, preferred_element_type=jnp.float32)
            return (input_tile.astype(jnp.float32) + gate[None, :] * projected).astype(jnp.bfloat16)

        def skip_tile():
            return input_tile
        return lax.cond(tile_active[tile_index], compute_tile, skip_tile)
    tiles = lax.map(one_tile, jnp.arange(TOKENS // TILE, dtype=jnp.int32))
    return tiles.reshape(TOKENS, D)
```

```python
import functools
import math

import jax
import jax.numpy as jnp
from jax import lax
from jax.experimental import pallas as pl
from jax.experimental.pallas import tpu as pltpu
from jax.sharding import PartitionSpec as P

HEAD_DIM = 128
MASKED = -1e30
LANES = 256
VMEM_BYTES = 48 << 20


def params():
    return pltpu.CompilerParams(vmem_limit_bytes=VMEM_BYTES)


def exchanged(block, axis):
    return lax.ppermute(block, axis, [(0, 1), (1, 0)])


def ring_order(count):
    return list(range(0, count, 2)) + list(range(count - 1, 0, -2))


def resident_kernel(flags_ref, fresh_ref, cache_ref, out_ref, held, sems):
    tiles, rows = held.shape[0], held.shape[1]
    width = held.shape[3]

    def copy(source, tile):
        return pltpu.make_async_copy(
            source.at[pl.ds(tile * rows, rows)], held.at[tile], sems.at[tile]
        )

    for tile in range(tiles):

        @pl.when(flags_ref[tile] != 0)
        def _(tile=tile):
            copy(fresh_ref, tile).start()

        @pl.when(flags_ref[tile] == 0)
        def _(tile=tile):
            copy(cache_ref, tile).start()

    to_row = lax.broadcasted_iota(jnp.int32, (2 * rows, 2 * rows), 0)
    from_row = lax.broadcasted_iota(jnp.int32, (2 * rows, 2 * rows), 1)
    wanted = jnp.where(to_row < rows, 2 * to_row, 2 * (to_row - rows) + 1)
    order = (from_row == wanted).astype(jnp.bfloat16)
    for tile in range(tiles):
        copy(fresh_ref, tile).wait()
        pairs = held[tile].reshape(2 * rows, width)
        sorted_rows = jnp.dot(order, pairs, preferred_element_type=jnp.float32)
        sorted_rows = sorted_rows.astype(jnp.bfloat16)
        out_ref[0, tile * rows : (tile + 1) * rows] = sorted_rows[:rows]
        out_ref[1, tile * rows : (tile + 1) * rows] = sorted_rows[rows:]


def resident_planes(flags, fresh, cache):
    tokens, _, width = fresh.shape
    tiles = flags.shape[0]
    rows = tokens // tiles
    return pl.pallas_call(
        resident_kernel,
        out_shape=jax.ShapeDtypeStruct((2, tokens, width), jnp.bfloat16),
        in_specs=[
            pl.BlockSpec(memory_space=pltpu.SMEM),
            pl.BlockSpec(memory_space=pl.ANY),
            pl.BlockSpec(memory_space=pl.ANY),
        ],
        out_specs=pl.BlockSpec(memory_space=pltpu.VMEM),
        scratch_shapes=[
            pltpu.VMEM((tiles, rows, 2, width), jnp.bfloat16),
            pltpu.SemaphoreType.DMA((tiles,)),
        ],
        compiler_params=params(),
        cost_estimate=pl.CostEstimate(
            flops=8 * tokens * rows * width, bytes_accessed=8 * tokens * width, transcendentals=0
        ),
        name="resident",
    )(flags, fresh, cache)


def attend_kernel(heads, mask_ref, q_ref, own_ref, other_ref, out_ref, bias_ref):
    tiles = mask_ref.shape[0]
    rows = q_ref.shape[0] // tiles
    keys = own_ref.shape[1]
    for side in range(2):
        for query in range(tiles):
            for key in range(tiles):
                bias_ref[side, query * rows : (query + 1) * rows, key * rows : (key + 1) * rows] = (
                    jnp.full((rows, rows), mask_ref[query, side * tiles + key], jnp.float32)
                )
    scale = math.log2(math.e) / math.sqrt(HEAD_DIM)
    contract_last = (((1,), (1,)), ((), ()))
    for head in range(heads):
        cols = slice(head * HEAD_DIM, (head + 1) * HEAD_DIM)
        query_head = q_ref[:, cols]
        scores = [
            lax.dot_general(
                query_head, ref[0, :, cols], contract_last, preferred_element_type=jnp.float32
            )
            * scale
            + bias_ref[side]
            for side, ref in enumerate((own_ref, other_ref))
        ]
        row_max = jnp.max(jnp.maximum(scores[0], scores[1]), axis=1, keepdims=True)
        terms = [jnp.exp2(part - row_max) for part in scores]
        total = jnp.sum(terms[0] + terms[1], axis=1, keepdims=True)
        summed = jnp.dot(
            terms[0].astype(jnp.bfloat16), own_ref[1, :, cols], preferred_element_type=jnp.float32
        ) + jnp.dot(
            terms[1].astype(jnp.bfloat16), other_ref[1, :, cols], preferred_element_type=jnp.float32
        )
        out_ref[:, cols] = (summed / total).astype(jnp.bfloat16)


def attended_heads(mask, queries, own, other, first, count, step):
    tokens = queries.shape[0]
    start = first // step
    width = step * HEAD_DIM
    kv_spec = pl.BlockSpec((2, tokens, width), lambda i: (0, 0, start + i))
    return pl.pallas_call(
        functools.partial(attend_kernel, step),
        grid=(count // step,),
        out_shape=jax.ShapeDtypeStruct((tokens, count * HEAD_DIM), jnp.bfloat16),
        in_specs=[
            pl.BlockSpec(memory_space=pltpu.SMEM),
            pl.BlockSpec((tokens, width), lambda i: (0, start + i)),
            kv_spec,
            kv_spec,
        ],
        out_specs=pl.BlockSpec((tokens, width), lambda i: (0, i)),
        scratch_shapes=[pltpu.VMEM((2, tokens, tokens), jnp.float32)],
        compiler_params=params(),
        cost_estimate=pl.CostEstimate(
            flops=8 * tokens * tokens * count * HEAD_DIM,
            bytes_accessed=12 * tokens * count * HEAD_DIM,
            transcendentals=2 * tokens * tokens * count,
        ),
        name="attend",
    )(mask, queries, own, other)


def project_kernel(pieces, halves, blocks, *refs):
    offsets_ref = refs[0]
    piece_refs = refs[1 : 1 + pieces]
    row_refs = refs[1 + pieces : 1 + pieces + halves * blocks]
    out_refs = refs[1 + pieces + halves * blocks : -2]
    weight, sems = refs[-2:]

    def copy(index):
        rows = piece_refs[index].shape[0]
        start = pl.multiple_of(offsets_ref[index], 16)
        return pltpu.make_async_copy(
            piece_refs[index], weight.at[pl.ds(start, rows)], sems.at[index]
        )

    for index in range(pieces):
        copy(index).start()
    for index in range(pieces):
        copy(index).wait()
    depth = weight.shape[0] // halves

    def one_step(step, _):
        cols = pl.ds(pl.multiple_of(step * LANES, LANES), LANES)
        for block in range(blocks):
            total = None
            for half in range(halves):
                part = jnp.dot(
                    row_refs[block * halves + half][...],
                    weight[half * depth : (half + 1) * depth, cols],
                    preferred_element_type=jnp.float32,
                )
                total = part if total is None else total + part
            rows = total.shape[0]
            if len(out_refs) == 1:
                out_refs[0][block * rows : (block + 1) * rows, cols] = total.astype(
                    out_refs[0].dtype
                )
            else:
                out_refs[block][:, cols] = total.astype(out_refs[block].dtype)
        return 0

    lax.fori_loop(0, weight.shape[1] // LANES, one_step, 0)


def projected_rows(offsets, pieces, row_blocks, out_shapes):
    halves = len(row_blocks[0])
    depth = halves * row_blocks[0][0].shape[1]
    cols = pieces[0].shape[1]
    rows = sum(parts[0].shape[0] for parts in row_blocks)
    vmem = pl.BlockSpec(memory_space=pltpu.VMEM)
    single = len(out_shapes) == 1
    result = pl.pallas_call(
        functools.partial(project_kernel, len(pieces), halves, len(row_blocks)),
        out_shape=out_shapes,
        in_specs=[pl.BlockSpec(memory_space=pltpu.SMEM)]
        + [pl.BlockSpec(memory_space=pl.ANY)] * len(pieces)
        + [vmem] * (halves * len(row_blocks)),
        out_specs=[vmem] * len(out_shapes),
        scratch_shapes=[
            pltpu.VMEM((depth, cols), jnp.bfloat16),
            pltpu.SemaphoreType.DMA((len(pieces),)),
        ],
        compiler_params=params(),
        cost_estimate=pl.CostEstimate(
            flops=2 * rows * depth * cols,
            bytes_accessed=2 * depth * (rows + cols) + 2 * rows * cols,
            transcendentals=0,
        ),
        name="project",
    )(offsets, *pieces, *[part for parts in row_blocks for part in parts])
    return result[0] if single else result


def finish_kernel(places_ref, flags_ref, input_ref, gate_ref, *refs):
    sources, out_ref = refs[:4], refs[-1]
    source = pl.program_id(0)
    tiles = flags_ref.shape[0]
    rows = out_ref.shape[0] // tiles
    for index in range(4):

        @pl.when(source == index)
        def _(index=index):
            for tile in range(tiles):
                span = slice(tile * rows, (tile + 1) * rows)

                @pl.when(flags_ref[tile] != 0)
                def _(span=span):
                    out_ref[span] = (
                        input_ref[span].astype(jnp.float32)
                        + gate_ref[...] * sources[index][span].astype(jnp.float32)
                    ).astype(jnp.bfloat16)

                @pl.when(flags_ref[tile] == 0)
                def _(span=span):
                    out_ref[span] = input_ref[span]


def finished(places, flags, block_input, gate, sources, offset, width, earlier):
    tokens, total = block_input.shape
    per_quarter = total // 4 // LANES
    start, steps = offset // LANES, width // LANES

    def wide(source, step, places, flags):
        return (0, places[source] * per_quarter + start + step)

    def narrow(index):
        def at(source, step, places, flags):
            return (0, jnp.where(source == index, step, jnp.where(source < index, 0, steps - 1)))

        return at

    in_specs = [
        pl.BlockSpec((tokens, LANES), wide),
        pl.BlockSpec((1, LANES), wide),
    ] + [pl.BlockSpec((tokens, LANES), narrow(index)) for index in range(4)]
    args = [block_input, gate[None], *sources]
    aliases = {}
    if earlier is not None:
        in_specs.append(pl.BlockSpec(memory_space=pl.ANY))
        args.append(earlier)
        aliases = {len(args) + 1: 0}
    return pl.pallas_call(
        finish_kernel,
        grid_spec=pltpu.PrefetchScalarGridSpec(
            num_scalar_prefetch=2,
            grid=(4, steps),
            in_specs=in_specs,
            out_specs=pl.BlockSpec((tokens, LANES), wide),
        ),
        out_shape=jax.ShapeDtypeStruct((tokens, total), jnp.bfloat16),
        input_output_aliases=aliases,
        compiler_params=params(),
        cost_estimate=pl.CostEstimate(
            flops=8 * tokens * width, bytes_accessed=24 * tokens * width, transcendentals=0
        ),
        name="finish",
    )(places, flags, *args)


def gathered(columns, position, order):
    count, rows = len(order), columns.shape[0]
    place = [0] * count
    for index, device in enumerate(order):
        place[device] = index
    place = jnp.array(place, jnp.int32)[position]
    order_table = jnp.array(order, jnp.int32)
    ahead = [(order[index], order[(index + 1) % count]) for index in range(count)]
    behind = [(to, start) for start, to in ahead]
    pieces, offsets = [columns], [position * rows]
    from_behind = from_ahead = columns
    for step in range(1, (count + 1) // 2):
        from_behind = lax.ppermute(from_behind, "fsdp", ahead)
        from_ahead = lax.ppermute(from_ahead, "fsdp", behind)
        pieces += [from_behind, from_ahead]
        offsets += [
            order_table[(place - step + count) % count] * rows,
            order_table[(place + step) % count] * rows,
        ]
    if count % 2 == 0:
        half = rows // 2
        opposite = order_table[(place + count // 2) % count] * rows
        pieces += [
            lax.ppermute(from_behind[:half], "fsdp", ahead),
            lax.ppermute(from_ahead[half:], "fsdp", behind),
        ]
        offsets += [opposite, opposite + half]
    return pieces, jnp.stack(offsets).astype(jnp.int32)


def local(
    block_input, gate, q_fresh, kv_fresh, kv_cache, active_list, active_count, key_list, out_weight
):
    part, position, side = (lax.axis_index(axis) for axis in ("groups", "fsdp", "blk"))
    positions = lax.axis_size("fsdp")
    tiles = active_list.shape[2]
    tokens, total = block_input.shape
    depth = q_fresh.shape[1]
    heads = depth // HEAD_DIM
    quarter = total // 4

    splits = (quarter,)
    ringed = positions == 8 and out_weight.shape[0] % 32 == 0
    weights, offset = [], 0
    for width in splits:
        columns = lax.dynamic_slice_in_dim(
            out_weight, (part * 2 + side) * quarter + offset, width, 1
        )
        if ringed:
            weights.append(gathered(columns, position, ring_order(positions)))
        else:
            whole = lax.all_gather(columns, "fsdp", axis=0, tiled=True)
            weights.append(([whole], jnp.zeros((1,), jnp.int32)))
        offset += width

    own_list, own_count = active_list[0, side], active_count[0, side]
    slots = jnp.arange(tiles, dtype=jnp.int32)
    flags = jnp.any(
        (own_list[:, None] == slots[None, :]) & (slots[:, None] < own_count), axis=0
    ).astype(jnp.int32)
    listed = lax.dynamic_slice_in_dim(key_list[0], side * tiles, tiles, 0)
    tile_ids = jnp.concatenate([side * tiles + slots, (1 - side) * tiles + slots])
    allowed = jnp.any(listed[:, :, None] == tile_ids[None, None, :], axis=1)
    mask = jnp.where(allowed, 0.0, MASKED).astype(jnp.float32)

    own_kv = resident_planes(flags, kv_fresh, kv_cache)
    other_kv = exchanged(own_kv, "blk")
    own_rows = [
        attended_heads(mask, q_fresh, own_kv, other_kv, first, heads // 2, heads // 4)
        for first in (0, heads // 2)
    ]
    far_rows = [exchanged(rows, "groups") for rows in own_rows]
    near_rows = [exchanged(rows, "blk") for rows in own_rows]
    far_near_rows = [exchanged(rows, "blk") for rows in far_rows]

    places = jnp.stack(
        [
            part * 2 + side,
            part * 2 + 1 - side,
            (1 - part) * 2 + side,
            (1 - part) * 2 + 1 - side,
        ]
    ).astype(jnp.int32)
    result, offset = None, 0
    for width, (pieces, offsets) in zip(splits, weights):
        one = jax.ShapeDtypeStruct((tokens, width), jnp.bfloat16)
        two = jax.ShapeDtypeStruct((2 * tokens, width), jnp.bfloat16)
        away = projected_rows(offsets, pieces, [far_rows, far_near_rows], [two])
        back = exchanged(away, "groups")
        own_part, near_part = projected_rows(offsets, pieces, [own_rows, near_rows], [one, one])
        sources = [
            own_part,
            exchanged(near_part, "blk"),
            back[:tokens],
            exchanged(back[tokens:], "blk"),
        ]
        result = finished(places, flags, block_input, gate, sources, offset, width, result)
        offset += width
    return result


def solution(mesh):
    in_specs = (
        P(("groups", "fsdp", "blk"), None),
        P("groups"),
        P(("groups", "fsdp", "blk"), None),
        P(("groups", "fsdp", "blk"), None, None),
        P(("groups", "fsdp", "blk"), None, None),
        P(("groups", "fsdp"), None, None),
        P(("groups", "fsdp"), None),
        P(("groups", "fsdp"), None, None),
        P("fsdp", None),
    )
    out_specs = P(("groups", "fsdp", "blk"), None)
    return jax.shard_map(local, mesh=mesh, in_specs=in_specs, out_specs=out_specs, check_vma=False)
```

```python
import functools
import math

import jax
import jax.numpy as jnp
from jax import lax
from jax.experimental import pallas as pl
from jax.experimental.pallas import tpu as pltpu
from jax.sharding import PartitionSpec as P

HEAD_DIM = 128
SPLIT = (3, 5)
MASKED = -1e30
ALL_VMEM = 62 << 20
SOME_VMEM = 24 << 20
SMEM = pl.BlockSpec(memory_space=pltpu.SMEM)
VMEM = pl.BlockSpec(memory_space=pltpu.VMEM)
HBM = pl.BlockSpec(memory_space=pltpu.HBM)


def params(limit):
    return pltpu.CompilerParams(vmem_limit_bytes=limit)


def exchanged(block, axis):
    return lax.ppermute(block, axis, [(0, 1), (1, 0)])


def ring_order(count):
    return list(range(0, count, 2)) + list(range(count - 1, 0, -2))


def ring_neighbour(position, shift, count):
    place = jnp.where(position % 2 == 0, position // 2, count - 1 - position // 2)
    place = (place + shift + count) % count
    return jnp.where(place < count // 2, 2 * place, 2 * (count - 1 - place) + 1)


def tile_active(list_ref, count_ref, side, tile):
    found = jnp.int32(0)
    for slot in range(list_ref.shape[2]):
        hit = (list_ref[0, side, slot] == tile) & (slot < count_ref[0, side])
        found = jnp.where(hit, 1, found)
    return found != 0


def attend_kernel(
    first,
    ids_ref,
    list_ref,
    count_ref,
    keys_ref,
    q_ref,
    own_fresh_ref,
    own_cache_ref,
    other_fresh_ref,
    other_cache_ref,
    out_ref,
    queries,
    pairs,
    key_rows,
    value_rows,
    bias,
    sems,
):
    spans, tokens, width = queries.shape
    tiles = list_ref.shape[2]
    rows = tokens // tiles
    own_side = ids_ref[2]
    sides = (own_side, 1 - own_side)
    sources = ((own_fresh_ref, own_cache_ref), (other_fresh_ref, other_cache_ref))

    def columns(span):
        return pl.ds(first + span * width, width)

    def load_queries(span):
        return pltpu.make_async_copy(
            q_ref.at[:, columns(span)], queries.at[span], sems.at[span, 2 * tiles]
        )

    def load_pairs(span, side, tile, source):
        index = side * tiles + tile
        return pltpu.make_async_copy(
            source.at[pl.ds(tile * rows, rows), :, columns(span)],
            pairs.at[span, index],
            sems.at[span, index],
        )

    for span in range(spans):
        load_queries(span).start()
        for side in range(2):
            for tile in range(tiles):
                active = tile_active(list_ref, count_ref, sides[side], tile)
                fresh, cache = sources[side]

                @pl.when(active)
                def _(span=span, side=side, tile=tile, source=fresh):
                    load_pairs(span, side, tile, source).start()

                @pl.when(jnp.logical_not(active))
                def _(span=span, side=side, tile=tile, source=cache):
                    load_pairs(span, side, tile, source).start()

    for query in range(tiles):
        for side in range(2):
            for key in range(tiles):
                allowed = jnp.int32(0)
                for slot in range(keys_ref.shape[2]):
                    hit = keys_ref[0, own_side * tiles + query, slot] == sides[side] * tiles + key
                    allowed = jnp.where(hit, 1, allowed)
                start = (side * tiles + key) * rows
                bias[query * rows : (query + 1) * rows, start : start + rows] = jnp.full(
                    (rows, rows), jnp.where(allowed != 0, 0.0, MASKED), jnp.float32
                )

    to_row = lax.broadcasted_iota(jnp.int32, (2 * rows, 2 * rows), 0)
    from_row = lax.broadcasted_iota(jnp.int32, (2 * rows, 2 * rows), 1)
    wanted = jnp.where(to_row < rows, 2 * to_row, 2 * (to_row - rows) + 1)
    order = (from_row == wanted).astype(jnp.bfloat16)
    scale = math.log2(math.e) / math.sqrt(HEAD_DIM)
    contract_last = (((1,), (1,)), ((), ()))
    for span in range(spans):
        for index in range(2 * tiles):
            load_pairs(span, index // tiles, index % tiles, own_fresh_ref).wait()
            sorted_rows = jnp.dot(
                order,
                pairs[span, index].reshape(2 * rows, width),
                preferred_element_type=jnp.float32,
            ).astype(jnp.bfloat16)
            key_rows[index * rows : (index + 1) * rows] = sorted_rows[:rows]
            value_rows[index * rows : (index + 1) * rows] = sorted_rows[rows:]
        load_queries(span).wait()
        for head in range(width // HEAD_DIM):
            cols = slice(head * HEAD_DIM, (head + 1) * HEAD_DIM)
            scores = lax.dot_general(
                queries[span, :, cols],
                key_rows[:, cols],
                contract_last,
                preferred_element_type=jnp.float32,
            )
            scores = scores * scale + bias[...]
            terms = jnp.exp2(scores - jnp.max(scores, axis=1, keepdims=True))
            total = jnp.sum(terms, axis=1, keepdims=True)
            summed = jnp.dot(
                terms.astype(jnp.bfloat16), value_rows[:, cols], preferred_element_type=jnp.float32
            )
            out_ref[:, span * width + cols.start : span * width + cols.stop] = (
                summed / total
            ).astype(jnp.bfloat16)


def attended_heads(ids, active_list, active_count, key_list, queries, pairs, first, width, spans):
    tokens = queries.shape[0]
    tiles = active_list.shape[2]
    rows = tokens // tiles
    span = width // spans
    return pl.pallas_call(
        functools.partial(attend_kernel, first),
        out_shape=jax.ShapeDtypeStruct((tokens, width), jnp.bfloat16),
        in_specs=[SMEM] * 4 + [HBM] * 5,
        out_specs=VMEM,
        scratch_shapes=[
            pltpu.VMEM((spans, tokens, span), jnp.bfloat16),
            pltpu.VMEM((spans, 2 * tiles, rows, 2, span), jnp.bfloat16),
            pltpu.VMEM((2 * tokens, span), jnp.bfloat16),
            pltpu.VMEM((2 * tokens, span), jnp.bfloat16),
            pltpu.VMEM((tokens, 2 * tokens), jnp.float32),
            pltpu.SemaphoreType.DMA((spans, 2 * tiles + 1)),
        ],
        compiler_params=params(ALL_VMEM),
        cost_estimate=pl.CostEstimate(flops=0, bytes_accessed=0, transcendentals=0),
        name="attend",
    )(ids, active_list, active_count, key_list, queries, *pairs)


def window(place, depth, columns):
    start = place * depth
    first = start // 128 * 128
    return pl.multiple_of(first, 128), pl.multiple_of(start - first, math.gcd(depth, 128))


def most_kernel(shifts, positions, splits, ids_ref, *refs):
    pieces, blocks = len(shifts), 4
    piece_refs, refs = refs[:pieces], refs[pieces:]
    row_refs, refs = refs[: blocks * len(splits)], refs[blocks * len(splits) :]
    sums, cuts, (weight, held, row_sems, sems) = refs[:2], refs[2:4], refs[4:]
    depth = piece_refs[0].shape[0]

    def load_piece(index):
        place = ring_neighbour(ids_ref[1], shifts[index], positions)
        start = pl.multiple_of(place * depth, math.gcd(depth, 64))
        return pltpu.make_async_copy(
            piece_refs[index], weight.at[pl.ds(start, depth)], sems.at[index]
        )

    def load_rows(block):
        copies, start = [], 0
        for index, width in enumerate(splits):
            copies.append(
                pltpu.make_async_copy(
                    row_refs[block * len(splits) + index],
                    held.at[block, :, pl.ds(start, width)],
                    row_sems.at[block, index],
                )
            )
            start += width
        return copies

    for copy in load_rows(0):
        copy.start()
    for index in range(pieces):
        load_piece(index).start()
    for block in range(1, blocks):
        for copy in load_rows(block):
            copy.start()
    missing = ring_neighbour(ids_ref[1], positions // 2, positions)
    start = pl.multiple_of(missing * depth, math.gcd(depth, 64))
    weight[pl.ds(start, depth)] = jnp.zeros((depth, weight.shape[1]), weight.dtype)
    for index in range(pieces):
        load_piece(index).wait()
    first, _ = window(missing, depth, held.shape[2])
    for block in range(blocks):
        for copy in load_rows(block):
            copy.wait()
        rows = held.shape[1]
        span = slice(block % 2 * rows, (block % 2 + 1) * rows)
        sums[block // 2][span] = jnp.dot(
            held[block], weight[...], preferred_element_type=jnp.float32
        )
        cuts[block // 2][span] = held[block, :, pl.ds(first, cuts[0].shape[1])]


def most_projected(ids, positions, pieces, shifts, row_blocks):
    rows, depth, cols = row_blocks[0][0].shape[0], pieces[0].shape[0], pieces[0].shape[1]
    splits = [part.shape[1] for part in row_blocks[0]]
    cut = -(-(depth + 64) // 128) * 128
    pair = jax.ShapeDtypeStruct((2 * rows, cols), jnp.float32)
    left = jax.ShapeDtypeStruct((2 * rows, cut), jnp.bfloat16)
    return pl.pallas_call(
        functools.partial(most_kernel, shifts, positions, splits),
        out_shape=[pair, pair, left, left],
        in_specs=[SMEM] + [HBM] * (len(pieces) + 4 * len(splits)),
        out_specs=[VMEM] * 4,
        scratch_shapes=[
            pltpu.VMEM((positions * depth, cols), jnp.bfloat16),
            pltpu.VMEM((4, rows, positions * depth), jnp.bfloat16),
            pltpu.SemaphoreType.DMA((4, len(splits))),
            pltpu.SemaphoreType.DMA((len(pieces),)),
        ],
        compiler_params=params(SOME_VMEM),
        cost_estimate=pl.CostEstimate(flops=0, bytes_accessed=0, transcendentals=0),
        name="project_most",
    )(ids, *pieces, *[part for block in row_blocks for part in block])


def last_kernel(positions, ids_ref, top_ref, bottom_ref, sums_ref, cut_ref, out_ref, weight):
    half = top_ref.shape[0]
    depth = 2 * half
    missing = ring_neighbour(ids_ref[1], positions // 2, positions)
    _, start = window(missing, depth, positions * depth)
    weight[...] = jnp.zeros(weight.shape, weight.dtype)
    weight[pl.ds(start, half)] = top_ref[...]
    weight[pl.ds(pl.multiple_of(start + half, math.gcd(half, 64)), half)] = bottom_ref[...]
    product = jnp.dot(cut_ref[...], weight[...], preferred_element_type=jnp.float32)
    out_ref[...] = (sums_ref[...] + product).astype(out_ref.dtype)


def last_projected(ids, positions, halves, sums, cut):
    return pl.pallas_call(
        functools.partial(last_kernel, positions),
        out_shape=jax.ShapeDtypeStruct(sums.shape, jnp.bfloat16),
        in_specs=[SMEM, VMEM, VMEM, VMEM, VMEM],
        out_specs=VMEM,
        scratch_shapes=[pltpu.VMEM((cut.shape[1], sums.shape[1]), jnp.bfloat16)],
        compiler_params=params(SOME_VMEM),
        cost_estimate=pl.CostEstimate(flops=0, bytes_accessed=0, transcendentals=0),
        name="project_last",
    )(ids, *halves, sums, cut)


def finish_kernel(
    from_parts, offset, firsts, ids_ref, list_ref, count_ref, gate_ref, input_ref, own_ref, near_ref, *refs
):
    out_ref, inputs, products, outputs, sems = refs[-5:]
    tokens, width = outputs.shape[1:]
    quarter = input_ref.shape[1] // 4
    tiles = list_ref.shape[2]
    rows = tokens // tiles
    part = ids_ref[0] if from_parts == 0 else 1 - ids_ref[0]
    side = ids_ref[2]

    def place(index):
        from_side = side if index == 0 else 1 - side
        start = (part * 2 + from_side) * quarter + offset
        return pl.ds(pl.multiple_of(start, 128), width)

    def loads(index):
        source, first = (own_ref, firsts[0]) if index == 0 else (near_ref, firsts[1])
        return (
            pltpu.make_async_copy(input_ref.at[:, place(index)], inputs.at[index], sems.at[0, index]),
            pltpu.make_async_copy(
                source.at[pl.ds(first, tokens)], products.at[index], sems.at[1, index]
            ),
        )

    def store(index):
        return pltpu.make_async_copy(outputs.at[index], out_ref.at[:, place(index)], sems.at[2, index])

    for index in range(2):
        for copy in loads(index):
            copy.start()
    for index in range(2):
        for copy in loads(index):
            copy.wait()
        gate = gate_ref[:, place(index)]
        for tile in range(tiles):
            span = slice(tile * rows, (tile + 1) * rows)
            active = tile_active(list_ref, count_ref, side, tile)

            @pl.when(active)
            def _(index=index, span=span, gate=gate):
                mixed = inputs[index, span].astype(jnp.float32)
                mixed = mixed + gate * products[index, span].astype(jnp.float32)
                outputs[index, span] = mixed.astype(jnp.bfloat16)

            @pl.when(jnp.logical_not(active))
            def _(index=index, span=span):
                outputs[index, span] = inputs[index, span]

        store(index).start()
    for index in range(2):
        store(index).wait()


def finished(ids, active_list, active_count, gate, block_input, own, near, firsts, from_parts, offset, earlier):
    tokens, total = block_input.shape
    width = own.shape[1]
    args = [ids, active_list, active_count, gate[None], block_input, own, near]
    in_specs = [SMEM, SMEM, SMEM, VMEM, HBM, HBM, HBM]
    aliases = {}
    if earlier is not None:
        aliases = {len(args): 0}
        args.append(earlier)
        in_specs.append(HBM)
    return pl.pallas_call(
        functools.partial(finish_kernel, from_parts, offset, firsts),
        in_specs=in_specs,
        out_specs=HBM,
        out_shape=jax.ShapeDtypeStruct((tokens, total), jnp.bfloat16),
        input_output_aliases=aliases,
        scratch_shapes=[pltpu.VMEM((2, tokens, width), jnp.bfloat16)] * 3
        + [pltpu.SemaphoreType.DMA((3, 2))],
        compiler_params=params(SOME_VMEM),
        cost_estimate=pl.CostEstimate(flops=0, bytes_accessed=0, transcendentals=0),
        name="finish",
    )(*args)


def after(value, *others):
    return lax.optimization_barrier((value, *others))[0]


def all_after(values, *others):
    return list(lax.optimization_barrier((*values, *others))[: len(values)])


def ring_steps(order):
    count = len(order)
    ahead = [(order[index], order[(index + 1) % count]) for index in range(count)]
    behind = [(to, start) for start, to in ahead]

    def step(held):
        return [lax.ppermute(held[0], "fsdp", ahead), lax.ppermute(held[1], "fsdp", behind)]

    def last_step(held):
        half = held[0].shape[0] // 2
        return step([held[0][:half], held[1][half:]])

    return step, last_step


def local(
    block_input, gate, q_fresh, kv_fresh, kv_cache, active_list, active_count, key_list, out_weight
):
    part, position, side = (lax.axis_index(axis) for axis in ("groups", "fsdp", "blk"))
    positions = lax.axis_size("fsdp")
    total = block_input.shape[1]
    heads = q_fresh.shape[1] // HEAD_DIM
    quarter = total // 4
    ids = jnp.stack([part, position, side]).astype(jnp.int32)

    first = quarter // 128 * SPLIT[0] // SPLIT[1] * 128
    widths = (first, quarter - first)
    ringed = positions == 8 and out_weight.shape[0] % 32 == 0
    columns = [
        lax.dynamic_slice_in_dim(out_weight, (part * 2 + side) * quarter + start, width, 1)
        for start, width in ((0, first), (first, quarter - first))
    ]

    pairs = [kv_fresh, kv_cache, exchanged(kv_fresh, "blk"), exchanged(kv_cache, "blk")]
    own_rows, start = [], 0
    for spans in (2, 2):
        width = heads // 4 * spans * HEAD_DIM
        own_rows.append(
            attended_heads(
                ids, active_list, active_count, key_list, q_fresh, pairs, start, width, spans
            )
        )
        start += width
    far_rows = [exchanged(rows, "groups") for rows in own_rows]

    def finish(index, own, near, from_parts, earlier):
        start = (0, first)[index]
        return finished(
            ids, active_list, active_count, gate, block_input, own, near, (0, tokens), from_parts, start, earlier
        )

    tokens = block_input.shape[0]
    if not ringed:
        near_rows = [exchanged(rows, "blk") for rows in own_rows]
        far_near_rows = [exchanged(rows, "blk") for rows in far_rows]
        result = None
        for index, block in enumerate(columns):
            whole = lax.all_gather(block, "fsdp", axis=0, tiled=True)
            for from_parts, row_blocks in enumerate(((own_rows, near_rows), (far_rows, far_near_rows))):
                rows = jnp.concatenate([jnp.concatenate(parts, axis=1) for parts in row_blocks])
                part_rows = jnp.dot(rows, whole, preferred_element_type=jnp.float32)
                part_rows = part_rows.astype(jnp.bfloat16)
                if from_parts == 1:
                    part_rows = exchanged(part_rows, "groups")
                result = finish(index, part_rows, exchanged(part_rows, "blk"), from_parts, result)
        return result

    step, last_step = ring_steps(ring_order(positions))

    def most(pieces):
        blocks = [far_rows, far_near_rows, own_rows, near_rows]
        return most_projected(ids, positions, pieces, (0, -1, 1, -2, 2, -3, 3), blocks)

    first_1, second_1 = step([columns[0]] * 2), step([columns[1]] * 2)
    first_2 = step(all_after(first_1, *second_1, own_rows[0]))
    first_3 = step(all_after(first_2, own_rows[1], far_rows[0]))
    first_4 = last_step(first_3)
    second_2 = step(all_after(second_1, *first_3))
    near_rows = [exchanged(rows, "blk") for rows in own_rows]
    far_near_rows = [exchanged(rows, "blk") for rows in far_rows]
    far_sums, own_sums, far_cut, own_cut = most([columns[0], *first_1, *first_2, *first_3])
    away = last_projected(ids, positions, first_4, far_sums, far_cut)
    back = exchanged(away, "groups")
    kept = last_projected(ids, positions, first_4, own_sums, own_cut)
    second_3 = step(all_after(second_2, away))
    second_4 = last_step(all_after(second_3, kept))
    far_sums, own_sums, far_cut, own_cut = most([columns[1], *second_1, *second_2, *second_3])
    away = last_projected(ids, positions, second_4, after(far_sums, back), far_cut)
    last_back = exchanged(away, "groups")
    result = finish(0, kept, exchanged(kept, "blk"), 0, None)
    kept = last_projected(ids, positions, second_4, own_sums, own_cut)
    result = finish(0, back, exchanged(back, "blk"), 1, result)
    result = finish(1, kept, exchanged(kept, "blk"), 0, result)
    last_back = after(last_back, result)
    return finish(1, last_back, exchanged(last_back, "blk"), 1, result)


def solution(mesh):
    in_specs = (
        P(("groups", "fsdp", "blk"), None),
        P("groups"),
        P(("groups", "fsdp", "blk"), None),
        P(("groups", "fsdp", "blk"), None, None),
        P(("groups", "fsdp", "blk"), None, None),
        P(("groups", "fsdp"), None, None),
        P(("groups", "fsdp"), None),
        P(("groups", "fsdp"), None, None),
        P("fsdp", None),
    )
    out_specs = P(("groups", "fsdp", "blk"), None)
    return jax.shard_map(local, mesh=mesh, in_specs=in_specs, out_specs=out_specs, check_vma=False)
```

```python
import functools
import math

import jax
import jax.numpy as jnp
from jax import lax
from jax.experimental import pallas as pl
from jax.experimental.pallas import tpu as pltpu
from jax.sharding import PartitionSpec as P

HEAD_DIM = 128
SPLIT = (7, 10)
MASKED = -1e30
ALL_VMEM = 62 << 20
SOME_VMEM = 24 << 20
SMEM = pl.BlockSpec(memory_space=pltpu.SMEM)
VMEM = pl.BlockSpec(memory_space=pltpu.VMEM)
HBM = pl.BlockSpec(memory_space=pltpu.HBM)


def params(limit):
    return pltpu.CompilerParams(vmem_limit_bytes=limit)


def exchanged(block, axis):
    return lax.ppermute(block, axis, [(0, 1), (1, 0)])


def ring_order(count):
    return list(range(0, count, 2)) + list(range(count - 1, 0, -2))


def ring_neighbour(position, shift, count):
    place = jnp.where(position % 2 == 0, position // 2, count - 1 - position // 2)
    place = (place + shift + count) % count
    return jnp.where(place < count // 2, 2 * place, 2 * (count - 1 - place) + 1)


def tile_active(list_ref, count_ref, side, tile):
    found = jnp.int32(0)
    for slot in range(list_ref.shape[2]):
        hit = (list_ref[0, side, slot] == tile) & (slot < count_ref[0, side])
        found = jnp.where(hit, 1, found)
    return found != 0


def attend_kernel(
    ids_ref,
    list_ref,
    count_ref,
    keys_ref,
    own_q_ref,
    other_q_ref,
    own_fresh_ref,
    own_cache_ref,
    other_fresh_ref,
    other_cache_ref,
    out_ref,
    queries,
    pairs,
    key_rows,
    value_rows,
    bias,
    sems,
):
    spans, _, tokens, width = queries.shape
    tiles = list_ref.shape[2]
    rows = tokens // tiles
    own_side = ids_ref[2]
    sides = (own_side, 1 - own_side)
    first = own_side * (spans * width)

    def columns(span):
        return pl.ds(pl.multiple_of(first + span * width, 128), width)

    def load_queries(span, side):
        source = (own_q_ref, other_q_ref)[side]
        return pltpu.make_async_copy(
            source.at[:, columns(span)], queries.at[span, side], sems.at[span, 2 * tiles + side]
        )

    def load_pairs(span, index, ref):
        return pltpu.make_async_copy(
            ref.at[pl.ds(index % tiles * rows, rows), :, columns(span)],
            pairs.at[span, index],
            sems.at[span, index],
        )

    for span in range(spans):
        for index in range(2 * tiles):
            active = tile_active(list_ref, count_ref, sides[index // tiles], index % tiles)
            fresh, cache = (
                (own_fresh_ref, own_cache_ref) if index < tiles else (other_fresh_ref, other_cache_ref)
            )

            @pl.when(active)
            def _(span=span, index=index, source=fresh):
                load_pairs(span, index, source).start()

            @pl.when(jnp.logical_not(active))
            def _(span=span, index=index, source=cache):
                load_pairs(span, index, source).start()

        for side in range(2):
            load_queries(span, side).start()

    for asking in range(2):
        for query in range(tiles):
            for side in range(2):
                for key in range(tiles):
                    allowed = jnp.int32(0)
                    for slot in range(keys_ref.shape[2]):
                        listed = keys_ref[0, sides[asking] * tiles + query, slot]
                        allowed = jnp.where(listed == sides[side] * tiles + key, 1, allowed)
                    start = (side * tiles + key) * rows
                    bias[asking, query * rows : (query + 1) * rows, start : start + rows] = jnp.full(
                        (rows, rows), jnp.where(allowed != 0, 0.0, MASKED), jnp.float32
                    )

    to_row = lax.broadcasted_iota(jnp.int32, (2 * rows, 2 * rows), 0)
    from_row = lax.broadcasted_iota(jnp.int32, (2 * rows, 2 * rows), 1)
    wanted = jnp.where(to_row < rows, 2 * to_row, 2 * (to_row - rows) + 1)
    order = (from_row == wanted).astype(jnp.bfloat16)
    scale = math.log2(math.e) / math.sqrt(HEAD_DIM)
    contract_last = (((1,), (1,)), ((), ()))
    for span in range(spans):
        for index in range(2 * tiles):
            load_pairs(span, index, own_fresh_ref).wait()
            sorted_rows = jnp.dot(
                order,
                pairs[span, index].reshape(2 * rows, width),
                preferred_element_type=jnp.float32,
            ).astype(jnp.bfloat16)
            key_rows[index * rows : (index + 1) * rows] = sorted_rows[:rows]
            value_rows[index * rows : (index + 1) * rows] = sorted_rows[rows:]
        for asking in range(2):
            load_queries(span, asking).wait()
            for head in range(width // HEAD_DIM):
                cols = slice(head * HEAD_DIM, (head + 1) * HEAD_DIM)
                scores = lax.dot_general(
                    queries[span, asking, :, cols],
                    key_rows[:, cols],
                    contract_last,
                    preferred_element_type=jnp.float32,
                )
                scores = scores * scale + bias[asking]
                terms = jnp.exp2(scores - jnp.max(scores, axis=1, keepdims=True))
                total = jnp.sum(terms, axis=1, keepdims=True)
                summed = jnp.dot(
                    terms.astype(jnp.bfloat16),
                    value_rows[:, cols],
                    preferred_element_type=jnp.float32,
                )
                out_ref[
                    asking * tokens : (asking + 1) * tokens,
                    span * width + cols.start : span * width + cols.stop,
                ] = (summed / total).astype(jnp.bfloat16)


def attended_heads(ids, active_list, active_count, key_list, queries, pairs):
    tokens, width = queries[0].shape[0], queries[0].shape[1] // 2
    tiles = active_list.shape[2]
    rows, spans = tokens // tiles, 2
    span = width // spans
    return pl.pallas_call(
        attend_kernel,
        out_shape=jax.ShapeDtypeStruct((2 * tokens, width), jnp.bfloat16),
        in_specs=[SMEM] * 4 + [HBM] * 6,
        out_specs=VMEM,
        scratch_shapes=[
            pltpu.VMEM((spans, 2, tokens, span), jnp.bfloat16),
            pltpu.VMEM((spans, 2 * tiles, rows, 2, span), jnp.bfloat16),
            pltpu.VMEM((2 * tokens, span), jnp.bfloat16),
            pltpu.VMEM((2 * tokens, span), jnp.bfloat16),
            pltpu.VMEM((2, tokens, 2 * tokens), jnp.float32),
            pltpu.SemaphoreType.DMA((spans, 2 * tiles + 2)),
        ],
        compiler_params=params(ALL_VMEM),
        cost_estimate=pl.CostEstimate(flops=0, bytes_accessed=0, transcendentals=0),
        name="attend",
    )(ids, active_list, active_count, key_list, *queries, *pairs)


def window(place, depth):
    start = place * depth
    first = start // 128 * 128
    return pl.multiple_of(first, 128), pl.multiple_of(start - first, math.gcd(depth, 128))


def most_kernel(shifts, starts, pairs, positions, ids_ref, *refs):
    pieces = len(shifts)
    piece_refs, row_refs, refs = refs[:pieces], refs[pieces:][: 2 * pairs], refs[pieces + 2 * pairs :]
    sums, cuts, (weight, held, row_sems, sems) = refs[:pairs], refs[pairs:][:pairs], refs[2 * pairs :]
    depth = piece_refs[0].shape[0]
    blocks, rows, width = held.shape
    side = ids_ref[2]
    halves = [pl.ds(pl.multiple_of(at * (width // 2), 128), width // 2) for at in (side, 1 - side)]

    def load_piece(index):
        place = ring_neighbour(ids_ref[1], shifts[index], positions)
        start = pl.multiple_of(place * depth, math.gcd(depth, 64))
        return pltpu.make_async_copy(
            piece_refs[index].at[:, pl.ds(starts[index], weight.shape[1])],
            weight.at[pl.ds(start, depth)],
            sems.at[index],
        )

    def load_rows(block):
        refs = row_refs[block // 2 * 2 : block // 2 * 2 + 2]
        places = (block % 2, 1 - block % 2)
        return [
            pltpu.make_async_copy(
                ref.at[pl.ds(place * rows, rows)], held.at[block, :, half], row_sems.at[block, index]
            )
            for index, (ref, place, half) in enumerate(zip(refs, places, halves))
        ]

    for copy in load_rows(0):
        copy.start()
    for index in range(pieces):
        load_piece(index).start()
    for block in range(1, blocks):
        for copy in load_rows(block):
            copy.start()
    missing = ring_neighbour(ids_ref[1], positions // 2, positions)
    start = pl.multiple_of(missing * depth, math.gcd(depth, 64))
    weight[pl.ds(start, depth)] = jnp.zeros((depth, weight.shape[1]), weight.dtype)
    for index in range(pieces):
        load_piece(index).wait()
    first, _ = window(missing, depth)
    for block in range(blocks):
        for copy in load_rows(block):
            copy.wait()
        span = slice(block % 2 * rows, (block % 2 + 1) * rows)
        sums[block // 2][span] = jnp.dot(
            held[block], weight[...], preferred_element_type=jnp.float32
        )
        cuts[block // 2][span] = held[block, :, pl.ds(first, cuts[0].shape[1])]


def most_projected(ids, positions, pieces, shifts, starts, cols, row_halves):
    depth, pairs = pieces[0].shape[0], len(row_halves) // 2
    rows = row_halves[0].shape[0] // 2
    cut = -(-(depth + 64) // 128) * 128
    return pl.pallas_call(
        functools.partial(most_kernel, shifts, starts, pairs, positions),
        out_shape=[jax.ShapeDtypeStruct((2 * rows, cols), jnp.float32)] * pairs
        + [jax.ShapeDtypeStruct((2 * rows, cut), jnp.bfloat16)] * pairs,
        in_specs=[SMEM] + [HBM] * (len(pieces) + 2 * pairs),
        out_specs=[VMEM] * (2 * pairs),
        scratch_shapes=[
            pltpu.VMEM((positions * depth, cols), jnp.bfloat16),
            pltpu.VMEM((2 * pairs, rows, positions * depth), jnp.bfloat16),
            pltpu.SemaphoreType.DMA((2 * pairs, 2)),
            pltpu.SemaphoreType.DMA((len(pieces),)),
        ],
        compiler_params=params(SOME_VMEM),
        cost_estimate=pl.CostEstimate(
            flops=4 * rows * pairs * depth * positions * cols, bytes_accessed=0, transcendentals=0
        ),
        name="project_most",
    )(ids, *pieces, *row_halves)


def last_kernel(positions, ids_ref, top_ref, bottom_ref, sums_ref, cut_ref, out_ref, weight):
    half = top_ref.shape[0]
    depth = 2 * half
    missing = ring_neighbour(ids_ref[1], positions // 2, positions)
    _, start = window(missing, depth)
    weight[...] = jnp.zeros(weight.shape, weight.dtype)
    weight[pl.ds(start, half)] = top_ref[...]
    weight[pl.ds(pl.multiple_of(start + half, math.gcd(half, 64)), half)] = bottom_ref[...]
    product = jnp.dot(cut_ref[...], weight[...], preferred_element_type=jnp.float32)
    out_ref[...] = (sums_ref[...] + product).astype(out_ref.dtype)


def last_projected(ids, positions, halves, sums, cut, flops):
    return pl.pallas_call(
        functools.partial(last_kernel, positions),
        out_shape=jax.ShapeDtypeStruct(sums.shape, jnp.bfloat16),
        in_specs=[SMEM, VMEM, VMEM, VMEM, VMEM],
        out_specs=VMEM,
        scratch_shapes=[pltpu.VMEM((cut.shape[1], sums.shape[1]), jnp.bfloat16)],
        compiler_params=params(SOME_VMEM),
        cost_estimate=pl.CostEstimate(flops=flops, bytes_accessed=0, transcendentals=0),
        name="project_last",
    )(ids, *halves, sums, cut)


def finish_kernel(
    from_parts, offset, firsts, ids_ref, list_ref, count_ref, gate_ref, input_ref, own_ref, near_ref, *refs
):
    out_ref, inputs, products, outputs, sems = refs[-5:]
    tokens, width = outputs.shape[1:]
    quarter = input_ref.shape[1] // 4
    tiles = list_ref.shape[2]
    rows = tokens // tiles
    part = ids_ref[0] if from_parts == 0 else 1 - ids_ref[0]
    side = ids_ref[2]

    def place(index):
        from_side = side if index == 0 else 1 - side
        start = (part * 2 + from_side) * quarter + offset
        return pl.ds(pl.multiple_of(start, 128), width)

    def loads(index):
        source, first = (own_ref, firsts[0]) if index == 0 else (near_ref, firsts[1])
        return (
            pltpu.make_async_copy(input_ref.at[:, place(index)], inputs.at[index], sems.at[0, index]),
            pltpu.make_async_copy(
                source.at[pl.ds(first, tokens)], products.at[index], sems.at[1, index]
            ),
        )

    def store(index):
        return pltpu.make_async_copy(outputs.at[index], out_ref.at[:, place(index)], sems.at[2, index])

    for index in range(2):
        for copy in loads(index):
            copy.start()
    for index in range(2):
        for copy in loads(index):
            copy.wait()
        gate = gate_ref[:, place(index)]
        for tile in range(tiles):
            span = slice(tile * rows, (tile + 1) * rows)
            active = tile_active(list_ref, count_ref, side, tile)

            @pl.when(active)
            def _(index=index, span=span, gate=gate):
                mixed = inputs[index, span].astype(jnp.float32)
                mixed = mixed + gate * products[index, span].astype(jnp.float32)
                outputs[index, span] = mixed.astype(jnp.bfloat16)

            @pl.when(jnp.logical_not(active))
            def _(index=index, span=span):
                outputs[index, span] = inputs[index, span]

        store(index).start()
    for index in range(2):
        store(index).wait()


def finished(ids, active_list, active_count, gate, block_input, own, near, firsts, from_parts, offset, earlier):
    tokens, total = block_input.shape
    width = own.shape[1]
    args = [ids, active_list, active_count, gate[None], block_input, own, near]
    in_specs = [SMEM, SMEM, SMEM, VMEM, HBM, HBM, HBM]
    aliases = {}
    if earlier is not None:
        aliases = {len(args): 0}
        args.append(earlier)
        in_specs.append(HBM)
    return pl.pallas_call(
        functools.partial(finish_kernel, from_parts, offset, firsts),
        in_specs=in_specs,
        out_specs=HBM,
        out_shape=jax.ShapeDtypeStruct((tokens, total), jnp.bfloat16),
        input_output_aliases=aliases,
        scratch_shapes=[pltpu.VMEM((2, tokens, width), jnp.bfloat16)] * 3
        + [pltpu.SemaphoreType.DMA((3, 2))],
        compiler_params=params(SOME_VMEM),
        cost_estimate=pl.CostEstimate(flops=3_000_000_000, bytes_accessed=0, transcendentals=0),
        name="finish",
    )(*args)


def after(value, *others):
    return lax.optimization_barrier((value, *others))[0]


def all_after(values, *others):
    return list(lax.optimization_barrier((*values, *others))[: len(values)])


def ring_steps(order):
    count = len(order)
    ahead = [(order[index], order[(index + 1) % count]) for index in range(count)]
    behind = [(to, start) for start, to in ahead]

    def step(held):
        return [lax.ppermute(held[0], "fsdp", ahead), lax.ppermute(held[1], "fsdp", behind)]

    def last_step(held):
        half = held[0].shape[0] // 2
        return step([held[0][:half], held[1][half:]])

    return step, last_step


def local(
    block_input, gate, q_fresh, kv_fresh, kv_cache, active_list, active_count, key_list, out_weight
):
    part, position, side = (lax.axis_index(axis) for axis in ("groups", "fsdp", "blk"))
    positions = lax.axis_size("fsdp")
    total = block_input.shape[1]
    heads = q_fresh.shape[1] // HEAD_DIM
    quarter = total // 4
    ids = jnp.stack([part, position, side]).astype(jnp.int32)

    first = quarter // 128 * SPLIT[0] // SPLIT[1] * 128
    ringed = positions == 8 and out_weight.shape[0] % 32 == 0
    columns = lax.dynamic_slice_in_dim(out_weight, (part * 2 + side) * quarter, quarter, 1)
    pairs = [kv_fresh, kv_cache, exchanged(kv_fresh, "blk"), exchanged(kv_cache, "blk")]
    queries = [q_fresh, exchanged(q_fresh, "blk")]
    own_rows = attended_heads(ids, active_list, active_count, key_list, queries, pairs)

    def finish(index, own, near, from_parts, earlier):
        start = (0, first)[index]
        return finished(
            ids, active_list, active_count, gate, block_input, own, near, (0, tokens), from_parts, start, earlier
        )

    tokens = block_input.shape[0]
    if not ringed:
        far_rows = exchanged(own_rows, "groups")
        near_rows, far_near_rows = exchanged(own_rows, "blk"), exchanged(far_rows, "blk")
        result = None
        for index, block in enumerate((columns[:, :first], columns[:, first:])):
            whole = lax.all_gather(block, "fsdp", axis=0, tiled=True)
            for from_parts, (mine, theirs) in enumerate(
                ((own_rows, near_rows), (far_rows, far_near_rows))
            ):
                theirs = jnp.concatenate([theirs[tokens:], theirs[:tokens]])
                low, high = jnp.where(side == 0, mine, theirs), jnp.where(side == 0, theirs, mine)
                rows = jnp.concatenate([low, high], axis=1)
                rows = jnp.dot(rows, whole, preferred_element_type=jnp.float32)
                rows = rows.astype(jnp.bfloat16)
                if from_parts == 1:
                    rows = exchanged(rows, "groups")
                result = finish(index, rows, exchanged(rows, "blk"), from_parts, result)
        return result

    step, last_step = ring_steps(ring_order(positions))

    def most(pieces, start, width, *row_halves):
        shifts, starts = (0, -1, 1, -2, 2, -3, 3), (start,) * 3 + (0,) * 4
        return most_projected(ids, positions, pieces, shifts, starts, width, row_halves)

    both_1 = step([columns] * 2)
    first_1 = [block[:, :first] for block in all_after(both_1, own_rows)]
    first_2 = step(first_1)
    first_3 = step(first_2)
    first_4 = last_step(first_3)
    far_rows = exchanged(own_rows, "groups")
    near_rows = exchanged(own_rows, "blk")
    far_near_rows = exchanged(after(far_rows, near_rows, *first_3), "blk")
    second_1 = [block[:, first:] for block in all_after(both_1, far_near_rows)]
    second_2 = step(second_1)
    pieces = [columns, *both_1, *first_2, *first_3]
    far_sums, far_cut = most(pieces, 0, first, far_rows, far_near_rows)
    away = last_projected(ids, positions, first_4, far_sums, far_cut, 0)
    back = exchanged(away, "groups")
    own_sums, own_cut = most(pieces, 0, first, after(own_rows, away), near_rows)
    kept = last_projected(ids, positions, first_4, own_sums, own_cut, 20_000_000_000)
    second_3 = step(all_after(second_2, away))
    second_4 = last_step(all_after(second_3, kept))
    result = finish(0, kept, exchanged(kept, "blk"), 0, None)
    pieces, rest = [columns, *both_1, *second_2, *second_3], quarter - first
    far_sums, own_sums, far_cut, own_cut = most(
        pieces, first, rest, far_rows, far_near_rows, own_rows, near_rows
    )
    away = last_projected(ids, positions, second_4, far_sums, far_cut, 0)
    last_back = exchanged(away, "groups")
    kept = last_projected(ids, positions, second_4, after(own_sums, away), own_cut, 20_000_000_000)
    back = after(back, *second_4)
    result = finish(0, back, exchanged(back, "blk"), 1, result)
    result = finish(1, kept, exchanged(kept, "blk"), 0, result)
    last_back = after(last_back, result)
    return finish(1, last_back, exchanged(last_back, "blk"), 1, result)


def solution(mesh):
    in_specs = (
        P(("groups", "fsdp", "blk"), None),
        P("groups"),
        P(("groups", "fsdp", "blk"), None),
        P(("groups", "fsdp", "blk"), None, None),
        P(("groups", "fsdp", "blk"), None, None),
        P(("groups", "fsdp"), None, None),
        P(("groups", "fsdp"), None),
        P(("groups", "fsdp"), None, None),
        P("fsdp", None),
    )
    out_specs = P(("groups", "fsdp", "blk"), None)
    return jax.shard_map(local, mesh=mesh, in_specs=in_specs, out_specs=out_specs, check_vma=False)
```

```python
import functools
import math

import jax
import jax.numpy as jnp
from jax import lax
from jax.experimental import pallas as pl
from jax.experimental.pallas import tpu as pltpu
from jax.sharding import PartitionSpec as P

HEAD_DIM = 128
SPLIT = (7, 10)
MASKED = -1e30
ALL_VMEM = 62 << 20
SOME_VMEM = 24 << 20
SMEM = pl.BlockSpec(memory_space=pltpu.SMEM)
VMEM = pl.BlockSpec(memory_space=pltpu.VMEM)
HBM = pl.BlockSpec(memory_space=pltpu.HBM)


def params(limit):
    return pltpu.CompilerParams(vmem_limit_bytes=limit)


def exchanged(block, axis):
    return lax.ppermute(block, axis, [(0, 1), (1, 0)])


def ring_order(count):
    return list(range(0, count, 2)) + list(range(count - 1, 0, -2))


def ring_neighbour(position, shift, count):
    place = jnp.where(position % 2 == 0, position // 2, count - 1 - position // 2)
    place = (place + shift + count) % count
    return jnp.where(place < count // 2, 2 * place, 2 * (count - 1 - place) + 1)


def tile_active(list_ref, count_ref, side, tile):
    found = jnp.int32(0)
    for slot in range(list_ref.shape[2]):
        hit = (list_ref[0, side, slot] == tile) & (slot < count_ref[0, side])
        found = jnp.where(hit, 1, found)
    return found != 0


def attend_kernel(
    ids_ref,
    list_ref,
    count_ref,
    keys_ref,
    own_q_ref,
    other_q_ref,
    own_fresh_ref,
    own_cache_ref,
    other_fresh_ref,
    other_cache_ref,
    out_ref,
    queries,
    pairs,
    key_rows,
    value_rows,
    bias,
    sems,
):
    spans, _, tokens, width = queries.shape
    tiles = list_ref.shape[2]
    rows = tokens // tiles
    own_side = ids_ref[2]
    sides = (own_side, 1 - own_side)
    first = own_side * (spans * width)

    def columns(span):
        return pl.ds(pl.multiple_of(first + span * width, 128), width)

    def load_queries(span, side):
        if side == 0:
            source = own_q_ref.at[:, columns(span)]
        else:
            source = other_q_ref.at[:, pl.ds(span * width, width)]
        return pltpu.make_async_copy(
            source, queries.at[span, side], sems.at[span, 2 * tiles + side]
        )

    def load_pairs(span, index, ref):
        return pltpu.make_async_copy(
            ref.at[pl.ds(index % tiles * rows, rows), :, columns(span)],
            pairs.at[span, index],
            sems.at[span, index],
        )

    for span in range(spans):
        for index in range(2 * tiles):
            active = tile_active(list_ref, count_ref, sides[index // tiles], index % tiles)
            fresh, cache = (
                (own_fresh_ref, own_cache_ref) if index < tiles else (other_fresh_ref, other_cache_ref)
            )

            @pl.when(active)
            def _(span=span, index=index, source=fresh):
                load_pairs(span, index, source).start()

            @pl.when(jnp.logical_not(active))
            def _(span=span, index=index, source=cache):
                load_pairs(span, index, source).start()

        for side in range(2):
            load_queries(span, side).start()

    for asking in range(2):
        for query in range(tiles):
            for side in range(2):
                for key in range(tiles):
                    allowed = jnp.int32(0)
                    for slot in range(keys_ref.shape[2]):
                        listed = keys_ref[0, sides[asking] * tiles + query, slot]
                        allowed = jnp.where(listed == sides[side] * tiles + key, 1, allowed)
                    start = (side * tiles + key) * rows
                    bias[asking, query * rows : (query + 1) * rows, start : start + rows] = jnp.full(
                        (rows, rows), jnp.where(allowed != 0, 0.0, MASKED), jnp.float32
                    )

    to_row = lax.broadcasted_iota(jnp.int32, (2 * rows, 2 * rows), 0)
    from_row = lax.broadcasted_iota(jnp.int32, (2 * rows, 2 * rows), 1)
    wanted = jnp.where(to_row < rows, 2 * to_row, 2 * (to_row - rows) + 1)
    order = (from_row == wanted).astype(jnp.bfloat16)
    scale = math.log2(math.e) / math.sqrt(HEAD_DIM)
    contract_last = (((1,), (1,)), ((), ()))
    for span in range(spans):
        for index in range(2 * tiles):
            load_pairs(span, index, own_fresh_ref).wait()
            sorted_rows = jnp.dot(
                order,
                pairs[span, index].reshape(2 * rows, width),
                preferred_element_type=jnp.float32,
            ).astype(jnp.bfloat16)
            key_rows[index * rows : (index + 1) * rows] = sorted_rows[:rows]
            value_rows[index * rows : (index + 1) * rows] = sorted_rows[rows:]
        for asking in range(2):
            load_queries(span, asking).wait()
            for head in range(width // HEAD_DIM):
                cols = slice(head * HEAD_DIM, (head + 1) * HEAD_DIM)
                scores = lax.dot_general(
                    queries[span, asking, :, cols],
                    key_rows[:, cols],
                    contract_last,
                    preferred_element_type=jnp.float32,
                )
                scores = scores * scale + bias[asking]
                terms = jnp.exp2(scores - jnp.max(scores, axis=1, keepdims=True))
                total = jnp.sum(terms, axis=1, keepdims=True)
                summed = jnp.dot(
                    terms.astype(jnp.bfloat16),
                    value_rows[:, cols],
                    preferred_element_type=jnp.float32,
                )
                out_ref[
                    asking * tokens : (asking + 1) * tokens,
                    span * width + cols.start : span * width + cols.stop,
                ] = (summed / total).astype(jnp.bfloat16)


def attended_heads(ids, active_list, active_count, key_list, queries, pairs):
    tokens, width = queries[0].shape[0], queries[0].shape[1] // 2
    tiles = active_list.shape[2]
    rows, spans = tokens // tiles, 2
    span = width // spans
    return pl.pallas_call(
        attend_kernel,
        out_shape=jax.ShapeDtypeStruct((2 * tokens, width), jnp.bfloat16),
        in_specs=[SMEM] * 4 + [HBM] * 6,
        out_specs=VMEM,
        scratch_shapes=[
            pltpu.VMEM((spans, 2, tokens, span), jnp.bfloat16),
            pltpu.VMEM((spans, 2 * tiles, rows, 2, span), jnp.bfloat16),
            pltpu.VMEM((2 * tokens, span), jnp.bfloat16),
            pltpu.VMEM((2 * tokens, span), jnp.bfloat16),
            pltpu.VMEM((2, tokens, 2 * tokens), jnp.float32),
            pltpu.SemaphoreType.DMA((spans, 2 * tiles + 2)),
        ],
        compiler_params=params(ALL_VMEM),
        cost_estimate=pl.CostEstimate(flops=0, bytes_accessed=0, transcendentals=0),
        name="attend",
    )(ids, active_list, active_count, key_list, *queries, *pairs)


def window(place, depth):
    start = place * depth
    first = start // 128 * 128
    return pl.multiple_of(first, 128), pl.multiple_of(start - first, math.gcd(depth, 128))


def most_kernel(shifts, starts, pairs, positions, ids_ref, *refs):
    pieces = len(shifts)
    piece_refs, row_refs, refs = refs[:pieces], refs[pieces:][: 2 * pairs], refs[pieces + 2 * pairs :]
    sums, cuts, (weight, held, row_sems, sems) = refs[:pairs], refs[pairs:][:pairs], refs[2 * pairs :]
    depth = piece_refs[0].shape[0]
    blocks, rows, width = held.shape
    side = ids_ref[2]
    halves = [pl.ds(pl.multiple_of(at * (width // 2), 128), width // 2) for at in (side, 1 - side)]

    def load_piece(index):
        place = ring_neighbour(ids_ref[1], shifts[index], positions)
        start = pl.multiple_of(place * depth, math.gcd(depth, 64))
        return pltpu.make_async_copy(
            piece_refs[index].at[:, pl.ds(starts[index], weight.shape[1])],
            weight.at[pl.ds(start, depth)],
            sems.at[index],
        )

    def load_rows(block):
        refs = row_refs[block // 2 * 2 : block // 2 * 2 + 2]
        places = (block % 2, 1 - block % 2)
        return [
            pltpu.make_async_copy(
                ref.at[pl.ds(place * rows, rows)], held.at[block, :, half], row_sems.at[block, index]
            )
            for index, (ref, place, half) in enumerate(zip(refs, places, halves))
        ]

    for copy in load_rows(0):
        copy.start()
    for index in range(pieces):
        load_piece(index).start()
    for block in range(1, blocks):
        for copy in load_rows(block):
            copy.start()
    missing = ring_neighbour(ids_ref[1], positions // 2, positions)
    start = pl.multiple_of(missing * depth, math.gcd(depth, 64))
    weight[pl.ds(start, depth)] = jnp.zeros((depth, weight.shape[1]), weight.dtype)
    for index in range(pieces):
        load_piece(index).wait()
    first, _ = window(missing, depth)
    for block in range(blocks):
        for copy in load_rows(block):
            copy.wait()
        span = slice(block % 2 * rows, (block % 2 + 1) * rows)
        sums[block // 2][span] = jnp.dot(
            held[block], weight[...], preferred_element_type=jnp.float32
        )
        cuts[block // 2][span] = held[block, :, pl.ds(first, cuts[0].shape[1])]


def most_projected(ids, positions, pieces, shifts, starts, cols, row_halves):
    depth, pairs = pieces[0].shape[0], len(row_halves) // 2
    rows = row_halves[0].shape[0] // 2
    cut = -(-(depth + 64) // 128) * 128
    return pl.pallas_call(
        functools.partial(most_kernel, shifts, starts, pairs, positions),
        out_shape=[jax.ShapeDtypeStruct((2 * rows, cols), jnp.float32)] * pairs
        + [jax.ShapeDtypeStruct((2 * rows, cut), jnp.bfloat16)] * pairs,
        in_specs=[SMEM] + [HBM] * (len(pieces) + 2 * pairs),
        out_specs=[VMEM] * (2 * pairs),
        scratch_shapes=[
            pltpu.VMEM((positions * depth, cols), jnp.bfloat16),
            pltpu.VMEM((2 * pairs, rows, positions * depth), jnp.bfloat16),
            pltpu.SemaphoreType.DMA((2 * pairs, 2)),
            pltpu.SemaphoreType.DMA((len(pieces),)),
        ],
        compiler_params=params(SOME_VMEM),
        cost_estimate=pl.CostEstimate(
            flops=4 * rows * pairs * depth * positions * cols, bytes_accessed=0, transcendentals=0
        ),
        name="project_most",
    )(ids, *pieces, *row_halves)


def last_kernel(positions, ids_ref, top_ref, bottom_ref, sums_ref, cut_ref, *refs):
    out_refs, weight = refs[:-1], refs[-1]
    half = top_ref.shape[0]
    depth = 2 * half
    missing = ring_neighbour(ids_ref[1], positions // 2, positions)
    _, start = window(missing, depth)
    weight[...] = jnp.zeros(weight.shape, weight.dtype)
    weight[pl.ds(start, half)] = top_ref[...]
    weight[pl.ds(pl.multiple_of(start + half, math.gcd(half, 64)), half)] = bottom_ref[...]
    rows = out_refs[0].shape[0]
    for index, out_ref in enumerate(out_refs):
        span = slice(index * rows, (index + 1) * rows)
        product = jnp.dot(cut_ref[span], weight[...], preferred_element_type=jnp.float32)
        out_ref[...] = (sums_ref[span] + product).astype(out_ref.dtype)


def last_projected(ids, positions, halves, sums, cut, flops, count=1):
    result = pl.pallas_call(
        functools.partial(last_kernel, positions),
        out_shape=[jax.ShapeDtypeStruct((sums.shape[0] // count, sums.shape[1]), jnp.bfloat16)]
        * count,
        in_specs=[SMEM, VMEM, VMEM, VMEM, VMEM],
        out_specs=[VMEM] * count,
        scratch_shapes=[pltpu.VMEM((cut.shape[1], sums.shape[1]), jnp.bfloat16)],
        compiler_params=params(SOME_VMEM),
        cost_estimate=pl.CostEstimate(flops=flops, bytes_accessed=0, transcendentals=0),
        name="project_last",
    )(ids, *halves, sums, cut)
    return result[0] if count == 1 else result


def finish_kernel(offset, places, ids_ref, list_ref, count_ref, gate_ref, input_ref, *refs):
    sources = refs[: len(places)]
    out_ref, inputs, products, outputs, sems = refs[-5:]
    tokens, width = outputs.shape[1:]
    quarter = input_ref.shape[1] // 4
    tiles = list_ref.shape[2]
    rows = tokens // tiles
    side = ids_ref[2]

    def columns(index):
        far, other, _ = places[index]
        of_part = 1 - ids_ref[0] if far else ids_ref[0]
        of_side = 1 - side if other else side
        start = (of_part * 2 + of_side) * quarter + offset
        return pl.ds(pl.multiple_of(start, 128), width)

    def loads(index):
        return (
            pltpu.make_async_copy(
                input_ref.at[:, columns(index)], inputs.at[index], sems.at[0, index]
            ),
            pltpu.make_async_copy(
                sources[index].at[pl.ds(places[index][2], tokens)],
                products.at[index],
                sems.at[1, index],
            ),
        )

    def store(index):
        return pltpu.make_async_copy(
            outputs.at[index], out_ref.at[:, columns(index)], sems.at[2, index]
        )

    for index in range(len(places)):
        for copy in loads(index):
            copy.start()
    for index in range(len(places)):
        for copy in loads(index):
            copy.wait()
        gate = gate_ref[:, columns(index)]
        for tile in range(tiles):
            span = slice(tile * rows, (tile + 1) * rows)
            active = tile_active(list_ref, count_ref, side, tile)

            @pl.when(active)
            def _(index=index, span=span, gate=gate):
                mixed = inputs[index, span].astype(jnp.float32)
                mixed = mixed + gate * products[index, span].astype(jnp.float32)
                outputs[index, span] = mixed.astype(jnp.bfloat16)

            @pl.when(jnp.logical_not(active))
            def _(index=index, span=span):
                outputs[index, span] = inputs[index, span]

        store(index).start()
    for index in range(len(places)):
        store(index).wait()


def finished(ids, active_list, active_count, gate, block_input, sources, places, offset, earlier):
    tokens, total = block_input.shape
    width, count = sources[0].shape[1], len(sources)
    args = [ids, active_list, active_count, gate[None], block_input, *sources]
    in_specs = [SMEM, SMEM, SMEM, VMEM, HBM] + [HBM] * count
    aliases = {}
    if earlier is not None:
        aliases = {len(args): 0}
        args.append(earlier)
        in_specs.append(HBM)
    return pl.pallas_call(
        functools.partial(finish_kernel, offset, places),
        in_specs=in_specs,
        out_specs=HBM,
        out_shape=jax.ShapeDtypeStruct((tokens, total), jnp.bfloat16),
        input_output_aliases=aliases,
        scratch_shapes=[pltpu.VMEM((count, tokens, width), jnp.bfloat16)] * 3
        + [pltpu.SemaphoreType.DMA((3, count))],
        compiler_params=params(SOME_VMEM),
        cost_estimate=pl.CostEstimate(
            flops=1_500_000_000 * count, bytes_accessed=0, transcendentals=0
        ),
        name="finish",
    )(*args)


def after(value, *others):
    return lax.optimization_barrier((value, *others))[0]


def all_after(values, *others):
    return list(lax.optimization_barrier((*values, *others))[: len(values)])


def ring_steps(order):
    count = len(order)
    ahead = [(order[index], order[(index + 1) % count]) for index in range(count)]
    behind = [(to, start) for start, to in ahead]

    def step(held):
        return [lax.ppermute(held[0], "fsdp", ahead), lax.ppermute(held[1], "fsdp", behind)]

    def last_step(held):
        half = held[0].shape[0] // 2
        return step([held[0][:half], held[1][half:]])

    return step, last_step


def local(
    block_input, gate, q_fresh, kv_fresh, kv_cache, active_list, active_count, key_list, out_weight
):
    part, position, side = (lax.axis_index(axis) for axis in ("groups", "fsdp", "blk"))
    positions = lax.axis_size("fsdp")
    total = block_input.shape[1]
    heads = q_fresh.shape[1] // HEAD_DIM
    quarter = total // 4
    ids = jnp.stack([part, position, side]).astype(jnp.int32)

    first = quarter // 128 * SPLIT[0] // SPLIT[1] * 128
    ringed = positions == 8 and out_weight.shape[0] % 32 == 0
    columns = lax.dynamic_slice_in_dim(out_weight, (part * 2 + side) * quarter, quarter, 1)
    pairs = [kv_fresh, kv_cache, exchanged(kv_fresh, "blk"), exchanged(kv_cache, "blk")]
    half = q_fresh.shape[1] // 2
    queries = [
        q_fresh,
        exchanged(lax.dynamic_slice_in_dim(q_fresh, (1 - side) * half, half, 1), "blk"),
    ]
    own_rows = attended_heads(ids, active_list, active_count, key_list, queries, pairs)

    def finish(index, sources, places, earlier):
        start = (0, first)[index]
        return finished(
            ids, active_list, active_count, gate, block_input, sources, places, start, earlier
        )

    tokens = block_input.shape[0]
    if not ringed:
        far_rows = exchanged(own_rows, "groups")
        near_rows, far_near_rows = exchanged(own_rows, "blk"), exchanged(far_rows, "blk")
        result = None
        for index, block in enumerate((columns[:, :first], columns[:, first:])):
            whole = lax.all_gather(block, "fsdp", axis=0, tiled=True)
            for from_parts, (mine, theirs) in enumerate(
                ((own_rows, near_rows), (far_rows, far_near_rows))
            ):
                theirs = jnp.concatenate([theirs[tokens:], theirs[:tokens]])
                low, high = jnp.where(side == 0, mine, theirs), jnp.where(side == 0, theirs, mine)
                rows = jnp.concatenate([low, high], axis=1)
                rows = jnp.dot(rows, whole, preferred_element_type=jnp.float32)
                rows = rows.astype(jnp.bfloat16)
                if from_parts == 1:
                    rows = exchanged(rows, "groups")
                sources = [rows, exchanged(rows, "blk")]
                places = ((from_parts, 0, 0), (from_parts, 1, tokens))
                result = finish(index, sources, places, result)
        return result

    step, last_step = ring_steps(ring_order(positions))

    def most(pieces, start, width, *row_halves):
        shifts, starts = (0, -1, 1, -2, 2, -3, 3), (start,) * 3 + (0,) * 4
        return most_projected(ids, positions, pieces, shifts, starts, width, row_halves)

    much = 20_000_000_000
    both_1 = step([columns] * 2)
    first_1 = [block[:, :first] for block in all_after(both_1, own_rows)]
    first_2 = step(first_1)
    first_3 = step(first_2)
    first_4 = last_step(first_3)
    far_rows = exchanged(own_rows, "groups")
    near_rows = exchanged(own_rows, "blk")
    far_near_rows = exchanged(after(far_rows, near_rows, *first_3), "blk")
    second_1 = [block[:, first:] for block in both_1]
    second_2 = step(all_after(second_1, far_rows))
    pieces = [columns, *both_1, *first_2, *first_3]
    far_sums, far_cut = most(pieces, 0, first, far_rows, far_near_rows)
    away = last_projected(ids, positions, first_4, far_sums, far_cut, 0)
    back = exchanged(away, "groups")
    own_sums, own_cut = most(pieces, 0, first, after(own_rows, away, *second_2), near_rows)
    kept = last_projected(ids, positions, first_4, own_sums, own_cut, much)
    second_3 = step(all_after(second_2, away))
    second_4 = last_step(all_after(second_3, kept))
    kept_near = exchanged(kept, "blk")
    pieces, rest = [columns, *both_1, *second_2, *second_3], quarter - first
    far_sums, far_cut = most(pieces, first, rest, far_rows, far_near_rows)
    away = last_projected(ids, positions, second_4, far_sums, far_cut, 0)
    last_back = exchanged(away, "groups")
    own_sums, own_cut = most(pieces, first, rest, after(own_rows, away), near_rows)
    rest_kept = last_projected(ids, positions, second_4, own_sums, own_cut, much)
    back = after(back, *second_4)
    result = finish(
        0,
        [kept, kept_near, back, exchanged(back, "blk")],
        ((0, 0, 0), (0, 1, tokens), (1, 0, 0), (1, 1, tokens)),
        None,
    )
    result = finish(
        1, [rest_kept, exchanged(rest_kept, "blk")], ((0, 0, 0), (0, 1, tokens)), result
    )
    last_back = after(last_back, result)
    last_near = exchanged(last_back, "blk")
    result = finish(1, [last_back], ((1, 0, 0),), result)
    return finish(1, [last_near], ((1, 1, tokens),), result)


def solution(mesh):
    in_specs = (
        P(("groups", "fsdp", "blk"), None),
        P("groups"),
        P(("groups", "fsdp", "blk"), None),
        P(("groups", "fsdp", "blk"), None, None),
        P(("groups", "fsdp", "blk"), None, None),
        P(("groups", "fsdp"), None, None),
        P(("groups", "fsdp"), None),
        P(("groups", "fsdp"), None, None),
        P("fsdp", None),
    )
    out_specs = P(("groups", "fsdp", "blk"), None)
    return jax.shard_map(local, mesh=mesh, in_specs=in_specs, out_specs=out_specs, check_vma=False)
```

```python
import functools
import math

import jax
import jax.numpy as jnp
from jax import lax
from jax.experimental import pallas as pl
from jax.experimental.pallas import tpu as pltpu
from jax.sharding import PartitionSpec as P

HEAD_DIM = 128
SPLIT = (7, 10)
MASKED = -1e30
ALL_VMEM = 62 << 20
SOME_VMEM = 24 << 20
SMEM = pl.BlockSpec(memory_space=pltpu.SMEM)
VMEM = pl.BlockSpec(memory_space=pltpu.VMEM)
HBM = pl.BlockSpec(memory_space=pltpu.HBM)


def params(limit):
    return pltpu.CompilerParams(vmem_limit_bytes=limit)


def exchanged(block, axis):
    return lax.ppermute(block, axis, [(0, 1), (1, 0)])


def ring_order(count):
    return list(range(0, count, 2)) + list(range(count - 1, 0, -2))


def ring_neighbour(position, shift, count):
    place = jnp.where(position % 2 == 0, position // 2, count - 1 - position // 2)
    place = (place + shift + count) % count
    return jnp.where(place < count // 2, 2 * place, 2 * (count - 1 - place) + 1)


def tile_active(list_ref, count_ref, side, tile):
    found = jnp.int32(0)
    for slot in range(list_ref.shape[2]):
        hit = (list_ref[0, side, slot] == tile) & (slot < count_ref[0, side])
        found = jnp.where(hit, 1, found)
    return found != 0


def attend_kernel(
    ids_ref,
    list_ref,
    count_ref,
    keys_ref,
    own_q_ref,
    other_q_ref,
    own_fresh_ref,
    own_cache_ref,
    other_fresh_ref,
    other_cache_ref,
    out_ref,
    queries,
    pairs,
    key_rows,
    value_rows,
    bias,
    sems,
):
    spans, tokens, width = queries.shape[0], queries.shape[1] // 2, queries.shape[2]
    tiles = list_ref.shape[2]
    rows = tokens // tiles
    own_side = ids_ref[2]
    sides = (own_side, 1 - own_side)
    first = own_side * (spans * width)

    def columns(span):
        return pl.ds(pl.multiple_of(first + span * width, 128), width)

    def load_queries(span, side):
        if side == 0:
            source = own_q_ref.at[:, columns(span)]
        else:
            source = other_q_ref.at[:, pl.ds(span * width, width)]
        return pltpu.make_async_copy(
            source,
            queries.at[span, pl.ds(side * tokens, tokens)],
            sems.at[span, 2 * tiles + side],
        )

    def load_pairs(span, index, ref):
        return pltpu.make_async_copy(
            ref.at[pl.ds(index % tiles * rows, rows), :, columns(span)],
            pairs.at[span, index],
            sems.at[span, index],
        )

    for span in range(spans):
        for index in range(2 * tiles):
            active = tile_active(list_ref, count_ref, sides[index // tiles], index % tiles)
            fresh, cache = (
                (own_fresh_ref, own_cache_ref) if index < tiles else (other_fresh_ref, other_cache_ref)
            )

            @pl.when(active)
            def _(span=span, index=index, source=fresh):
                load_pairs(span, index, source).start()

            @pl.when(jnp.logical_not(active))
            def _(span=span, index=index, source=cache):
                load_pairs(span, index, source).start()

        for side in range(2):
            load_queries(span, side).start()

    for asking in range(2):
        for query in range(tiles):
            for side in range(2):
                for key in range(tiles):
                    allowed = jnp.int32(0)
                    for slot in range(keys_ref.shape[2]):
                        listed = keys_ref[0, sides[asking] * tiles + query, slot]
                        allowed = jnp.where(listed == sides[side] * tiles + key, 1, allowed)
                    start = (side * tiles + key) * rows
                    at = (asking * tiles + query) * rows
                    bias[at : at + rows, start : start + rows] = jnp.full(
                        (rows, rows), jnp.where(allowed != 0, 0.0, MASKED), jnp.float32
                    )

    to_row = lax.broadcasted_iota(jnp.int32, (2 * rows, 2 * rows), 0)
    from_row = lax.broadcasted_iota(jnp.int32, (2 * rows, 2 * rows), 1)
    wanted = jnp.where(to_row < rows, 2 * to_row, 2 * (to_row - rows) + 1)
    order = (from_row == wanted).astype(jnp.bfloat16)
    scale = math.log2(math.e) / math.sqrt(HEAD_DIM)
    contract_last = (((1,), (1,)), ((), ()))
    for span in range(spans):
        for index in range(2 * tiles):
            load_pairs(span, index, own_fresh_ref).wait()
            sorted_rows = jnp.dot(
                order,
                pairs[span, index].reshape(2 * rows, width),
                preferred_element_type=jnp.float32,
            ).astype(jnp.bfloat16)
            key_rows[index * rows : (index + 1) * rows] = sorted_rows[:rows]
            value_rows[index * rows : (index + 1) * rows] = sorted_rows[rows:]
        for asking in range(2):
            load_queries(span, asking).wait()
        for head in range(width // HEAD_DIM):
            cols = slice(head * HEAD_DIM, (head + 1) * HEAD_DIM)
            scores = lax.dot_general(
                queries[span, :, cols],
                key_rows[:, cols],
                contract_last,
                preferred_element_type=jnp.float32,
            )
            scores = scores * scale + bias[...]
            terms = jnp.exp2(scores - jnp.max(scores, axis=1, keepdims=True))
            total = jnp.sum(terms, axis=1, keepdims=True)
            summed = jnp.dot(
                terms.astype(jnp.bfloat16), value_rows[:, cols], preferred_element_type=jnp.float32
            )
            out_ref[:, span * width + cols.start : span * width + cols.stop] = (
                summed / total
            ).astype(jnp.bfloat16)


def attended_heads(ids, active_list, active_count, key_list, queries, pairs):
    tokens, width = queries[0].shape[0], queries[0].shape[1] // 2
    tiles = active_list.shape[2]
    rows, spans = tokens // tiles, 2
    span = width // spans
    return pl.pallas_call(
        attend_kernel,
        out_shape=jax.ShapeDtypeStruct((2 * tokens, width), jnp.bfloat16),
        in_specs=[SMEM] * 4 + [HBM] * 6,
        out_specs=VMEM,
        scratch_shapes=[
            pltpu.VMEM((spans, 2 * tokens, span), jnp.bfloat16),
            pltpu.VMEM((spans, 2 * tiles, rows, 2, span), jnp.bfloat16),
            pltpu.VMEM((2 * tokens, span), jnp.bfloat16),
            pltpu.VMEM((2 * tokens, span), jnp.bfloat16),
            pltpu.VMEM((2 * tokens, 2 * tokens), jnp.float32),
            pltpu.SemaphoreType.DMA((spans, 2 * tiles + 2)),
        ],
        compiler_params=params(ALL_VMEM),
        cost_estimate=pl.CostEstimate(flops=0, bytes_accessed=0, transcendentals=0),
        name="attend",
    )(ids, active_list, active_count, key_list, *queries, *pairs)


def window(place, depth):
    start = place * depth
    first = start // 128 * 128
    return pl.multiple_of(first, 128), pl.multiple_of(start - first, math.gcd(depth, 128))


def most_kernel(shifts, starts, pairs, positions, whole, ids_ref, *refs):
    pieces = len(shifts)
    piece_refs, row_refs, refs = refs[:pieces], refs[pieces:][: 2 * pairs], refs[pieces + 2 * pairs :]
    sums, cuts, (weight, held, row_sems, sems) = refs[:pairs], refs[pairs:-4], refs[-4:]
    depth = piece_refs[0].shape[0]
    blocks, rows, width = held.shape
    side = ids_ref[2]
    halves = [pl.ds(pl.multiple_of(at * (width // 2), 128), width // 2) for at in (side, 1 - side)]

    def load_piece(index):
        piece = piece_refs[index].shape[0]
        later = piece if index == positions else 0
        start = ring_neighbour(ids_ref[1], shifts[index], positions) * depth + later
        start = pl.multiple_of(start, math.gcd(piece, 64))
        return pltpu.make_async_copy(
            piece_refs[index].at[:, pl.ds(starts[index], weight.shape[1])],
            weight.at[pl.ds(start, piece)],
            sems.at[index],
        )

    def load_rows(block):
        refs = row_refs[block // 2 * 2 : block // 2 * 2 + 2]
        places = (block % 2, 1 - block % 2)
        return [
            pltpu.make_async_copy(
                ref.at[pl.ds(place * rows, rows)], held.at[block, :, half], row_sems.at[block, index]
            )
            for index, (ref, place, half) in enumerate(zip(refs, places, halves))
        ]

    for copy in load_rows(0):
        copy.start()
    for index in range(pieces):
        load_piece(index).start()
    for block in range(1, blocks):
        for copy in load_rows(block):
            copy.start()
    missing = ring_neighbour(ids_ref[1], positions // 2, positions)
    if not whole:
        start = pl.multiple_of(missing * depth, math.gcd(depth, 64))
        weight[pl.ds(start, depth)] = jnp.zeros((depth, weight.shape[1]), weight.dtype)
    for index in range(pieces):
        load_piece(index).wait()
    first, _ = window(missing, depth)
    for block in range(blocks):
        for copy in load_rows(block):
            copy.wait()
        span = slice(block % 2 * rows, (block % 2 + 1) * rows)
        sums[block // 2][span] = jnp.dot(
            held[block], weight[...], preferred_element_type=jnp.float32
        ).astype(sums[0].dtype)
        if not whole:
            cuts[block // 2][span] = held[block, :, pl.ds(first, cuts[0].shape[1])]


def most_projected(ids, positions, pieces, shifts, starts, cols, row_halves):
    depth, pairs = pieces[0].shape[0], len(row_halves) // 2
    rows = row_halves[0].shape[0] // 2
    cut, whole = -(-(depth + 64) // 128) * 128, len(pieces) > positions
    sums = jax.ShapeDtypeStruct((2 * rows, cols), jnp.bfloat16 if whole else jnp.float32)
    cuts = [] if whole else [jax.ShapeDtypeStruct((2 * rows, cut), jnp.bfloat16)] * pairs
    return pl.pallas_call(
        functools.partial(most_kernel, shifts, starts, pairs, positions, whole),
        out_shape=[sums] * pairs + cuts,
        in_specs=[SMEM] + [HBM] * (len(pieces) + 2 * pairs),
        out_specs=[VMEM] * (pairs + len(cuts)),
        scratch_shapes=[
            pltpu.VMEM((positions * depth, cols), jnp.bfloat16),
            pltpu.VMEM((2 * pairs, rows, positions * depth), jnp.bfloat16),
            pltpu.SemaphoreType.DMA((2 * pairs, 2)),
            pltpu.SemaphoreType.DMA((len(pieces),)),
        ],
        compiler_params=params(SOME_VMEM),
        cost_estimate=pl.CostEstimate(
            flops=22_000_000_000 if whole else 4 * rows * pairs * depth * positions * cols,
            bytes_accessed=0,
            transcendentals=0,
        ),
        name="project_most",
    )(ids, *pieces, *row_halves)


def last_kernel(positions, ids_ref, top_ref, bottom_ref, sums_ref, cut_ref, *refs):
    out_refs, weight = refs[:-1], refs[-1]
    half = top_ref.shape[0]
    depth = 2 * half
    missing = ring_neighbour(ids_ref[1], positions // 2, positions)
    _, start = window(missing, depth)
    weight[...] = jnp.zeros(weight.shape, weight.dtype)
    weight[pl.ds(start, half)] = top_ref[...]
    weight[pl.ds(pl.multiple_of(start + half, math.gcd(half, 64)), half)] = bottom_ref[...]
    rows = out_refs[0].shape[0]
    for index, out_ref in enumerate(out_refs):
        span = slice(index * rows, (index + 1) * rows)
        product = jnp.dot(cut_ref[span], weight[...], preferred_element_type=jnp.float32)
        out_ref[...] = (sums_ref[span] + product).astype(out_ref.dtype)


def last_projected(ids, positions, halves, sums, cut, flops, count=1):
    result = pl.pallas_call(
        functools.partial(last_kernel, positions),
        out_shape=[jax.ShapeDtypeStruct((sums.shape[0] // count, sums.shape[1]), jnp.bfloat16)]
        * count,
        in_specs=[SMEM, VMEM, VMEM, VMEM, VMEM],
        out_specs=[VMEM] * count,
        scratch_shapes=[pltpu.VMEM((cut.shape[1], sums.shape[1]), jnp.bfloat16)],
        compiler_params=params(SOME_VMEM),
        cost_estimate=pl.CostEstimate(flops=flops, bytes_accessed=0, transcendentals=0),
        name="project_last",
    )(ids, *halves, sums, cut)
    return result[0] if count == 1 else result


def finish_kernel(places, ids_ref, list_ref, count_ref, gate_ref, input_ref, *refs):
    sources = refs[: len(places)]
    out_ref, inputs, products, outputs, sems = refs[-5:]
    tokens = outputs.shape[1]
    widths = [source.shape[1] for source in sources]
    quarter = input_ref.shape[1] // 4
    tiles = list_ref.shape[2]
    rows = tokens // tiles
    side = ids_ref[2]

    def columns(index):
        far, other, _, offset = places[index]
        of_part = 1 - ids_ref[0] if far else ids_ref[0]
        of_side = 1 - side if other else side
        start = (of_part * 2 + of_side) * quarter + offset
        return pl.ds(pl.multiple_of(start, 128), widths[index])

    def loads(index):
        return (
            pltpu.make_async_copy(
                input_ref.at[:, columns(index)], inputs.at[index, :, pl.ds(0, widths[index])], sems.at[0, index]
            ),
            pltpu.make_async_copy(
                sources[index].at[pl.ds(places[index][2], tokens)],
                products.at[index, :, pl.ds(0, widths[index])],
                sems.at[1, index],
            ),
        )

    def store(index):
        return pltpu.make_async_copy(
            outputs.at[index, :, pl.ds(0, widths[index])],
            out_ref.at[:, columns(index)],
            sems.at[2, index],
        )

    for index in range(len(places)):
        for copy in loads(index):
            copy.start()
    for index in range(len(places)):
        for copy in loads(index):
            copy.wait()
        gate, cols = gate_ref[:, columns(index)], slice(0, widths[index])
        for tile in range(tiles):
            span = slice(tile * rows, (tile + 1) * rows)
            active = tile_active(list_ref, count_ref, side, tile)

            @pl.when(active)
            def _(index=index, span=span, cols=cols, gate=gate):
                mixed = inputs[index, span, cols].astype(jnp.float32)
                mixed = mixed + gate * products[index, span, cols].astype(jnp.float32)
                outputs[index, span, cols] = mixed.astype(jnp.bfloat16)

            @pl.when(jnp.logical_not(active))
            def _(index=index, span=span, cols=cols):
                outputs[index, span, cols] = inputs[index, span, cols]

        store(index).start()
    for index in range(len(places)):
        store(index).wait()


def finished(ids, active_list, active_count, gate, block_input, sources, places, earlier):
    tokens, total = block_input.shape
    width, count = max(source.shape[1] for source in sources), len(sources)
    args = [ids, active_list, active_count, gate[None], block_input, *sources]
    in_specs = [SMEM, SMEM, SMEM, VMEM, HBM] + [HBM] * count
    aliases = {}
    if earlier is not None:
        aliases = {len(args): 0}
        args.append(earlier)
        in_specs.append(HBM)
    return pl.pallas_call(
        functools.partial(finish_kernel, places),
        in_specs=in_specs,
        out_specs=HBM,
        out_shape=jax.ShapeDtypeStruct((tokens, total), jnp.bfloat16),
        input_output_aliases=aliases,
        scratch_shapes=[pltpu.VMEM((count, tokens, width), jnp.bfloat16)] * 3
        + [pltpu.SemaphoreType.DMA((3, count))],
        compiler_params=params(SOME_VMEM),
        cost_estimate=pl.CostEstimate(
            flops=1_500_000_000 * count, bytes_accessed=0, transcendentals=0
        ),
        name="finish",
    )(*args)


def after(value, *others):
    return lax.optimization_barrier((value, *others))[0]


def all_after(values, *others):
    return list(lax.optimization_barrier((*values, *others))[: len(values)])


def ring_steps(order):
    count = len(order)
    ahead = [(order[index], order[(index + 1) % count]) for index in range(count)]
    behind = [(to, start) for start, to in ahead]

    def step(held):
        return [lax.ppermute(held[0], "fsdp", ahead), lax.ppermute(held[1], "fsdp", behind)]

    def last_step(held):
        half = held[0].shape[0] // 2
        return step([held[0][:half], held[1][half:]])

    return step, last_step


def local(
    block_input, gate, q_fresh, kv_fresh, kv_cache, active_list, active_count, key_list, out_weight
):
    part, position, side = (lax.axis_index(axis) for axis in ("groups", "fsdp", "blk"))
    positions = lax.axis_size("fsdp")
    total = block_input.shape[1]
    heads = q_fresh.shape[1] // HEAD_DIM
    quarter = total // 4
    ids = jnp.stack([part, position, side]).astype(jnp.int32)

    first = quarter // 128 * SPLIT[0] // SPLIT[1] * 128
    ringed = positions == 8 and out_weight.shape[0] % 32 == 0
    columns = lax.dynamic_slice_in_dim(out_weight, (part * 2 + side) * quarter, quarter, 1)
    pairs = [kv_fresh, kv_cache, exchanged(kv_fresh, "blk"), exchanged(kv_cache, "blk")]
    half = q_fresh.shape[1] // 2
    queries = [
        q_fresh,
        exchanged(lax.dynamic_slice_in_dim(q_fresh, (1 - side) * half, half, 1), "blk"),
    ]
    own_rows = attended_heads(ids, active_list, active_count, key_list, queries, pairs)

    def finish(sources, places, earlier):
        return finished(ids, active_list, active_count, gate, block_input, sources, places, earlier)

    tokens = block_input.shape[0]
    if not ringed:
        far_rows = exchanged(own_rows, "groups")
        near_rows, far_near_rows = exchanged(own_rows, "blk"), exchanged(far_rows, "blk")
        result = None
        for index, block in enumerate((columns[:, :first], columns[:, first:])):
            whole = lax.all_gather(block, "fsdp", axis=0, tiled=True)
            for from_parts, (mine, theirs) in enumerate(
                ((own_rows, near_rows), (far_rows, far_near_rows))
            ):
                theirs = jnp.concatenate([theirs[tokens:], theirs[:tokens]])
                low, high = jnp.where(side == 0, mine, theirs), jnp.where(side == 0, theirs, mine)
                rows = jnp.concatenate([low, high], axis=1)
                rows = jnp.dot(rows, whole, preferred_element_type=jnp.float32)
                rows = rows.astype(jnp.bfloat16)
                if from_parts == 1:
                    rows = exchanged(rows, "groups")
                sources = [rows, exchanged(rows, "blk")]
                start = (0, first)[index]
                places = ((from_parts, 0, 0, start), (from_parts, 1, tokens, start))
                result = finish(sources, places, result)
        return result

    step, last_step = ring_steps(ring_order(positions))

    def most(pieces, start, width, *row_halves):
        shifts = (0, -1, 1, -2, 2, -3, 3, 4, 4)[: len(pieces)]
        starts = ((start,) * 3 + (0,) * 6)[: len(pieces)]
        return most_projected(ids, positions, pieces, shifts, starts, width, row_halves)

    both_1 = step([columns] * 2)
    first_1 = [block[:, :first] for block in all_after(both_1, own_rows)]
    first_2 = step(first_1)
    first_3 = step(first_2)
    first_4 = last_step(first_3)
    far_rows = exchanged(own_rows, "groups")
    near_rows = exchanged(own_rows, "blk")
    far_near_rows = exchanged(after(far_rows, near_rows, *first_3), "blk")
    second_1 = [block[:, first:] for block in both_1]
    second_2 = step(all_after(second_1, far_rows))
    pieces = [columns, *both_1, *first_2, *first_3]
    far_sums, far_cut = most(pieces, 0, first, far_rows, far_near_rows)
    away = last_projected(ids, positions, first_4, far_sums, far_cut, 0)
    back = exchanged(away, "groups")
    (kept,) = most(
        [*pieces, *first_4], 0, first, after(own_rows, away, *second_2), near_rows
    )
    second_3 = step(all_after(second_2, away))
    second_4 = last_step(all_after(second_3, kept))
    kept_near = exchanged(kept, "blk")
    pieces, rest = [columns, *both_1, *second_2, *second_3], quarter - first
    far_sums, far_cut = most(pieces, first, rest, far_rows, far_near_rows)
    away = last_projected(ids, positions, second_4, far_sums, far_cut, 0)
    last_back = exchanged(away, "groups")
    (rest_kept,) = most(
        [*pieces, *second_4], first, rest, after(own_rows, away), near_rows
    )
    back = after(back, *second_4)
    result = finish(
        [kept, kept_near, back, exchanged(back, "blk")],
        ((0, 0, 0, 0), (0, 1, tokens, 0), (1, 0, 0, 0), (1, 1, tokens, 0)),
        None,
    )
    result = finish(
        [rest_kept, exchanged(rest_kept, "blk")],
        ((0, 0, 0, first), (0, 1, tokens, first)),
        result,
    )
    last_back = after(last_back, result)
    last_near = exchanged(last_back, "blk")
    result = finish([last_back], ((1, 0, 0, first),), result)
    return finish([last_near], ((1, 1, tokens, first),), result)


def solution(mesh):
    in_specs = (
        P(("groups", "fsdp", "blk"), None),
        P("groups"),
        P(("groups", "fsdp", "blk"), None),
        P(("groups", "fsdp", "blk"), None, None),
        P(("groups", "fsdp", "blk"), None, None),
        P(("groups", "fsdp"), None, None),
        P(("groups", "fsdp"), None),
        P(("groups", "fsdp"), None, None),
        P("fsdp", None),
    )
    out_specs = P(("groups", "fsdp", "blk"), None)
    return jax.shard_map(local, mesh=mesh, in_specs=in_specs, out_specs=out_specs, check_vma=False)
```

```python
import functools
import math

import jax
import jax.numpy as jnp
from jax import lax
from jax.experimental import pallas as pl
from jax.experimental.pallas import tpu as pltpu
from jax.sharding import PartitionSpec as P

HEAD_DIM = 128
SPLIT = (7, 10)
MASKED = -1e30
ALL_VMEM = 62 << 20
SOME_VMEM = 24 << 20
SMEM = pl.BlockSpec(memory_space=pltpu.SMEM)
VMEM = pl.BlockSpec(memory_space=pltpu.VMEM)
HBM = pl.BlockSpec(memory_space=pltpu.HBM)


def params(limit):
    return pltpu.CompilerParams(vmem_limit_bytes=limit)


def exchanged(block, axis):
    return lax.ppermute(block, axis, [(0, 1), (1, 0)])


def ring_order(count):
    return list(range(0, count, 2)) + list(range(count - 1, 0, -2))


def ring_neighbour(position, shift, count):
    place = jnp.where(position % 2 == 0, position // 2, count - 1 - position // 2)
    place = (place + shift + count) % count
    return jnp.where(place < count // 2, 2 * place, 2 * (count - 1 - place) + 1)


def tile_active(list_ref, count_ref, side, tile):
    found = jnp.int32(0)
    for slot in range(list_ref.shape[2]):
        hit = (list_ref[0, side, slot] == tile) & (slot < count_ref[0, side])
        found = jnp.where(hit, 1, found)
    return found != 0


def attend_kernel(
    ids_ref,
    list_ref,
    count_ref,
    keys_ref,
    own_q_ref,
    other_q_ref,
    own_fresh_ref,
    own_cache_ref,
    other_fresh_ref,
    other_cache_ref,
    out_ref,
    queries,
    pairs,
    key_rows,
    value_rows,
    bias,
    sems,
):
    spans, tokens, width = queries.shape[0], queries.shape[1] // 2, queries.shape[2]
    tiles = list_ref.shape[2]
    rows = tokens // tiles
    own_side = ids_ref[2]
    sides = (own_side, 1 - own_side)
    first = own_side * (spans * width)

    def columns(span):
        return pl.ds(pl.multiple_of(first + span * width, 128), width)

    def load_queries(span, side):
        if side == 0:
            source = own_q_ref.at[:, columns(span)]
        else:
            source = other_q_ref.at[:, pl.ds(span * width, width)]
        return pltpu.make_async_copy(
            source,
            queries.at[span, pl.ds(side * tokens, tokens)],
            sems.at[span, 2 * tiles + side],
        )

    def load_pairs(span, index, ref):
        return pltpu.make_async_copy(
            ref.at[pl.ds(index % tiles * rows, rows), :, columns(span)],
            pairs.at[span, index],
            sems.at[span, index],
        )

    for span in range(spans):
        for index in range(2 * tiles):
            active = tile_active(list_ref, count_ref, sides[index // tiles], index % tiles)
            fresh, cache = (
                (own_fresh_ref, own_cache_ref) if index < tiles else (other_fresh_ref, other_cache_ref)
            )

            @pl.when(active)
            def _(span=span, index=index, source=fresh):
                load_pairs(span, index, source).start()

            @pl.when(jnp.logical_not(active))
            def _(span=span, index=index, source=cache):
                load_pairs(span, index, source).start()

        for side in range(2):
            load_queries(span, side).start()

    for asking in range(2):
        for query in range(tiles):
            for side in range(2):
                for key in range(tiles):
                    allowed = jnp.int32(0)
                    for slot in range(keys_ref.shape[2]):
                        listed = keys_ref[0, sides[asking] * tiles + query, slot]
                        allowed = jnp.where(listed == sides[side] * tiles + key, 1, allowed)
                    start = (side * tiles + key) * rows
                    at = (asking * tiles + query) * rows
                    bias[at : at + rows, start : start + rows] = jnp.full(
                        (rows, rows), jnp.where(allowed != 0, 0.0, MASKED), jnp.float32
                    )

    to_row = lax.broadcasted_iota(jnp.int32, (2 * rows, 2 * rows), 0)
    from_row = lax.broadcasted_iota(jnp.int32, (2 * rows, 2 * rows), 1)
    wanted = jnp.where(to_row < rows, 2 * to_row, 2 * (to_row - rows) + 1)
    order = (from_row == wanted).astype(jnp.bfloat16)
    scale = math.log2(math.e) / math.sqrt(HEAD_DIM)
    contract_last = (((1,), (1,)), ((), ()))
    for span in range(spans):
        for index in range(2 * tiles):
            load_pairs(span, index, own_fresh_ref).wait()
            sorted_rows = jnp.dot(
                order,
                pairs[span, index].reshape(2 * rows, width),
                preferred_element_type=jnp.float32,
            ).astype(jnp.bfloat16)
            key_rows[index * rows : (index + 1) * rows] = sorted_rows[:rows]
            value_rows[index * rows : (index + 1) * rows] = sorted_rows[rows:]
        for asking in range(2):
            load_queries(span, asking).wait()
        for head in range(width // HEAD_DIM):
            cols = slice(head * HEAD_DIM, (head + 1) * HEAD_DIM)
            scores = lax.dot_general(
                queries[span, :, cols],
                key_rows[:, cols],
                contract_last,
                preferred_element_type=jnp.float32,
            )
            scores = scores * scale + bias[...]
            terms = jnp.exp2(scores - jnp.max(scores, axis=1, keepdims=True))
            total = jnp.sum(terms, axis=1, keepdims=True)
            summed = jnp.dot(
                terms.astype(jnp.bfloat16), value_rows[:, cols], preferred_element_type=jnp.float32
            )
            out_ref[:, span * width + cols.start : span * width + cols.stop] = (
                summed / total
            ).astype(jnp.bfloat16)


def attended_heads(ids, active_list, active_count, key_list, queries, pairs):
    tokens, width = queries[0].shape[0], queries[0].shape[1] // 2
    tiles = active_list.shape[2]
    rows, spans = tokens // tiles, 2
    span = width // spans
    return pl.pallas_call(
        attend_kernel,
        out_shape=jax.ShapeDtypeStruct((2 * tokens, width), jnp.bfloat16),
        in_specs=[SMEM] * 4 + [HBM] * 6,
        out_specs=VMEM,
        scratch_shapes=[
            pltpu.VMEM((spans, 2 * tokens, span), jnp.bfloat16),
            pltpu.VMEM((spans, 2 * tiles, rows, 2, span), jnp.bfloat16),
            pltpu.VMEM((2 * tokens, span), jnp.bfloat16),
            pltpu.VMEM((2 * tokens, span), jnp.bfloat16),
            pltpu.VMEM((2 * tokens, 2 * tokens), jnp.float32),
            pltpu.SemaphoreType.DMA((spans, 2 * tiles + 2)),
        ],
        compiler_params=params(ALL_VMEM),
        cost_estimate=pl.CostEstimate(flops=0, bytes_accessed=0, transcendentals=0),
        name="attend",
    )(ids, active_list, active_count, key_list, *queries, *pairs)


def window(place, depth):
    start = place * depth
    first = start // 128 * 128
    return pl.multiple_of(first, 128), pl.multiple_of(start - first, math.gcd(depth, 128))


def most_kernel(shifts, starts, pairs, positions, whole, ids_ref, *refs):
    pieces = len(shifts)
    piece_refs, row_refs, refs = refs[:pieces], refs[pieces:][: 2 * pairs], refs[pieces + 2 * pairs :]
    sums, cuts, (weight, held, row_sems, sems) = refs[:pairs], refs[pairs:-4], refs[-4:]
    depth = piece_refs[0].shape[0]
    blocks, rows, width = held.shape
    side = ids_ref[2]
    halves = [pl.ds(pl.multiple_of(at * (width // 2), 128), width // 2) for at in (side, 1 - side)]

    def load_piece(index):
        piece = piece_refs[index].shape[0]
        later = piece if index == positions else 0
        start = ring_neighbour(ids_ref[1], shifts[index], positions) * depth + later
        start = pl.multiple_of(start, math.gcd(piece, 64))
        return pltpu.make_async_copy(
            piece_refs[index].at[:, pl.ds(starts[index], weight.shape[1])],
            weight.at[pl.ds(start, piece)],
            sems.at[index],
        )

    def load_rows(block):
        refs = row_refs[block // 2 * 2 : block // 2 * 2 + 2]
        places = (block % 2, 1 - block % 2)
        return [
            pltpu.make_async_copy(
                ref.at[pl.ds(place * rows, rows)], held.at[block, :, half], row_sems.at[block, index]
            )
            for index, (ref, place, half) in enumerate(zip(refs, places, halves))
        ]

    for copy in load_rows(0):
        copy.start()
    for index in range(pieces):
        load_piece(index).start()
    for block in range(1, blocks):
        for copy in load_rows(block):
            copy.start()
    missing = ring_neighbour(ids_ref[1], positions // 2, positions)
    if not whole:
        start = pl.multiple_of(missing * depth, math.gcd(depth, 64))
        weight[pl.ds(start, depth)] = jnp.zeros((depth, weight.shape[1]), weight.dtype)
    for index in range(pieces):
        load_piece(index).wait()
    first, _ = window(missing, depth)
    for block in range(blocks):
        for copy in load_rows(block):
            copy.wait()
        span = slice(block % 2 * rows, (block % 2 + 1) * rows)
        sums[block // 2][span] = jnp.dot(
            held[block], weight[...], preferred_element_type=jnp.float32
        ).astype(sums[0].dtype)
        if not whole:
            cuts[block // 2][span] = held[block, :, pl.ds(first, cuts[0].shape[1])]


def most_projected(ids, positions, pieces, shifts, starts, cols, row_halves):
    depth, pairs = pieces[0].shape[0], len(row_halves) // 2
    rows = row_halves[0].shape[0] // 2
    cut, whole = -(-(depth + 64) // 128) * 128, len(pieces) > positions
    sums = jax.ShapeDtypeStruct((2 * rows, cols), jnp.bfloat16 if whole else jnp.float32)
    cuts = [] if whole else [jax.ShapeDtypeStruct((2 * rows, cut), jnp.bfloat16)] * pairs
    return pl.pallas_call(
        functools.partial(most_kernel, shifts, starts, pairs, positions, whole),
        out_shape=[sums] * pairs + cuts,
        in_specs=[SMEM] + [HBM] * (len(pieces) + 2 * pairs),
        out_specs=[VMEM] * (pairs + len(cuts)),
        scratch_shapes=[
            pltpu.VMEM((positions * depth, cols), jnp.bfloat16),
            pltpu.VMEM((2 * pairs, rows, positions * depth), jnp.bfloat16),
            pltpu.SemaphoreType.DMA((2 * pairs, 2)),
            pltpu.SemaphoreType.DMA((len(pieces),)),
        ],
        compiler_params=params(SOME_VMEM),
        cost_estimate=pl.CostEstimate(
            flops=22_000_000_000 if whole else 4 * rows * pairs * depth * positions * cols,
            bytes_accessed=0,
            transcendentals=0,
        ),
        name="project_most",
    )(ids, *pieces, *row_halves)


def last_kernel(positions, ids_ref, top_ref, bottom_ref, sums_ref, cut_ref, *refs):
    out_refs, weight = refs[:-1], refs[-1]
    half = top_ref.shape[0]
    depth = 2 * half
    missing = ring_neighbour(ids_ref[1], positions // 2, positions)
    _, start = window(missing, depth)
    weight[...] = jnp.zeros(weight.shape, weight.dtype)
    weight[pl.ds(start, half)] = top_ref[...]
    weight[pl.ds(pl.multiple_of(start + half, math.gcd(half, 64)), half)] = bottom_ref[...]
    rows = out_refs[0].shape[0]
    for index, out_ref in enumerate(out_refs):
        span = slice(index * rows, (index + 1) * rows)
        product = jnp.dot(cut_ref[span], weight[...], preferred_element_type=jnp.float32)
        out_ref[...] = (sums_ref[span] + product).astype(out_ref.dtype)


def last_projected(ids, positions, halves, sums, cut, flops, count=1):
    result = pl.pallas_call(
        functools.partial(last_kernel, positions),
        out_shape=[jax.ShapeDtypeStruct((sums.shape[0] // count, sums.shape[1]), jnp.bfloat16)]
        * count,
        in_specs=[SMEM, VMEM, VMEM, VMEM, VMEM],
        out_specs=[VMEM] * count,
        scratch_shapes=[pltpu.VMEM((cut.shape[1], sums.shape[1]), jnp.bfloat16)],
        compiler_params=params(SOME_VMEM),
        cost_estimate=pl.CostEstimate(flops=flops, bytes_accessed=0, transcendentals=0),
        name="project_last",
    )(ids, *halves, sums, cut)
    return result[0] if count == 1 else result


def finish_kernel(places, ids_ref, list_ref, count_ref, gate_ref, input_ref, *refs):
    sources = refs[: len(places)]
    out_ref, inputs, products, outputs, sems = refs[-5:]
    tokens = outputs.shape[1]
    widths = [source.shape[1] for source in sources]
    quarter = input_ref.shape[1] // 4
    tiles = list_ref.shape[2]
    rows = tokens // tiles
    side = ids_ref[2]

    def columns(index):
        far, other, _, offset = places[index]
        of_part = 1 - ids_ref[0] if far else ids_ref[0]
        of_side = 1 - side if other else side
        start = (of_part * 2 + of_side) * quarter + offset
        return pl.ds(pl.multiple_of(start, 128), widths[index])

    def loads(index):
        return (
            pltpu.make_async_copy(
                input_ref.at[:, columns(index)], inputs.at[index, :, pl.ds(0, widths[index])], sems.at[0, index]
            ),
            pltpu.make_async_copy(
                sources[index].at[pl.ds(places[index][2], tokens)],
                products.at[index, :, pl.ds(0, widths[index])],
                sems.at[1, index],
            ),
        )

    def store(index):
        return pltpu.make_async_copy(
            outputs.at[index, :, pl.ds(0, widths[index])],
            out_ref.at[:, columns(index)],
            sems.at[2, index],
        )

    for index in range(len(places)):
        for copy in loads(index):
            copy.start()
    for index in range(len(places)):
        for copy in loads(index):
            copy.wait()
        gate, cols = gate_ref[:, columns(index)], slice(0, widths[index])
        for tile in range(tiles):
            span = slice(tile * rows, (tile + 1) * rows)
            active = tile_active(list_ref, count_ref, side, tile)

            @pl.when(active)
            def _(index=index, span=span, cols=cols, gate=gate):
                mixed = inputs[index, span, cols].astype(jnp.float32)
                mixed = mixed + gate * products[index, span, cols].astype(jnp.float32)
                outputs[index, span, cols] = mixed.astype(jnp.bfloat16)

            @pl.when(jnp.logical_not(active))
            def _(index=index, span=span, cols=cols):
                outputs[index, span, cols] = inputs[index, span, cols]

        store(index).start()
    for index in range(len(places)):
        store(index).wait()


def finished(ids, active_list, active_count, gate, block_input, sources, places, earlier):
    tokens, total = block_input.shape
    width, count = max(source.shape[1] for source in sources), len(sources)
    args = [ids, active_list, active_count, gate[None], block_input, *sources]
    in_specs = [SMEM, SMEM, SMEM, VMEM, HBM] + [HBM] * count
    aliases = {}
    if earlier is not None:
        aliases = {len(args): 0}
        args.append(earlier)
        in_specs.append(HBM)
    return pl.pallas_call(
        functools.partial(finish_kernel, places),
        in_specs=in_specs,
        out_specs=HBM,
        out_shape=jax.ShapeDtypeStruct((tokens, total), jnp.bfloat16),
        input_output_aliases=aliases,
        scratch_shapes=[pltpu.VMEM((count, tokens, width), jnp.bfloat16)] * 3
        + [pltpu.SemaphoreType.DMA((3, count))],
        compiler_params=params(SOME_VMEM),
        cost_estimate=pl.CostEstimate(
            flops=1_500_000_000 * count, bytes_accessed=0, transcendentals=0
        ),
        name="finish",
    )(*args)


def after(value, *others):
    return lax.optimization_barrier((value, *others))[0]


def all_after(values, *others):
    return list(lax.optimization_barrier((*values, *others))[: len(values)])


def ring_steps(order):
    count = len(order)
    ahead = [(order[index], order[(index + 1) % count]) for index in range(count)]
    behind = [(to, start) for start, to in ahead]

    def step(held):
        return [lax.ppermute(held[0], "fsdp", ahead), lax.ppermute(held[1], "fsdp", behind)]

    def last_step(held):
        half = held[0].shape[0] // 2
        return step([held[0][:half], held[1][half:]])

    return step, last_step


def local(
    block_input, gate, q_fresh, kv_fresh, kv_cache, active_list, active_count, key_list, out_weight
):
    part, position, side = (lax.axis_index(axis) for axis in ("groups", "fsdp", "blk"))
    positions = lax.axis_size("fsdp")
    total = block_input.shape[1]
    heads = q_fresh.shape[1] // HEAD_DIM
    quarter = total // 4
    ids = jnp.stack([part, position, side]).astype(jnp.int32)

    first = quarter // 128 * SPLIT[0] // SPLIT[1] * 128
    ringed = positions == 8 and out_weight.shape[0] % 32 == 0
    columns = lax.dynamic_slice_in_dim(out_weight, (part * 2 + side) * quarter, quarter, 1)
    pairs = [kv_fresh, kv_cache, exchanged(kv_fresh, "blk"), exchanged(kv_cache, "blk")]
    half = q_fresh.shape[1] // 2
    queries = [
        q_fresh,
        exchanged(lax.dynamic_slice_in_dim(q_fresh, (1 - side) * half, half, 1), "blk"),
    ]
    own_rows = attended_heads(ids, active_list, active_count, key_list, queries, pairs)

    def finish(sources, places, earlier):
        return finished(ids, active_list, active_count, gate, block_input, sources, places, earlier)

    tokens = block_input.shape[0]
    if not ringed:
        far_rows = exchanged(own_rows, "groups")
        near_rows, far_near_rows = exchanged(own_rows, "blk"), exchanged(far_rows, "blk")
        result = None
        for index, block in enumerate((columns[:, :first], columns[:, first:])):
            whole = lax.all_gather(block, "fsdp", axis=0, tiled=True)
            for from_parts, (mine, theirs) in enumerate(
                ((own_rows, near_rows), (far_rows, far_near_rows))
            ):
                theirs = jnp.concatenate([theirs[tokens:], theirs[:tokens]])
                low, high = jnp.where(side == 0, mine, theirs), jnp.where(side == 0, theirs, mine)
                rows = jnp.concatenate([low, high], axis=1)
                rows = jnp.dot(rows, whole, preferred_element_type=jnp.float32)
                rows = rows.astype(jnp.bfloat16)
                if from_parts == 1:
                    rows = exchanged(rows, "groups")
                sources = [rows, exchanged(rows, "blk")]
                start = (0, first)[index]
                places = ((from_parts, 0, 0, start), (from_parts, 1, tokens, start))
                result = finish(sources, places, result)
        return result

    step, last_step = ring_steps(ring_order(positions))

    def most(pieces, start, width, *row_halves):
        shifts = (0, -1, 1, -2, 2, -3, 3, 4, 4)[: len(pieces)]
        starts = ((start,) * 3 + (0,) * 6)[: len(pieces)]
        return most_projected(ids, positions, pieces, shifts, starts, width, row_halves)

    both_1 = step([columns] * 2)
    first_1 = [block[:, :first] for block in all_after(both_1, own_rows)]
    first_2 = step(first_1)
    first_3 = step(first_2)
    first_4 = last_step(first_3)
    far_rows = exchanged(own_rows, "groups")
    near_rows = exchanged(own_rows, "blk")
    far_near_rows = exchanged(after(far_rows, near_rows, *first_3), "blk")
    second_1 = [block[:, first:] for block in both_1]
    second_2 = step(all_after(second_1, far_rows))
    pieces = [columns, *both_1, *first_2, *first_3]
    far_sums, far_cut = most(pieces, 0, first, far_rows, far_near_rows)
    away = last_projected(ids, positions, first_4, far_sums, far_cut, 0)
    back = exchanged(away, "groups")
    (kept,) = most(
        [*pieces, *first_4], 0, first, after(own_rows, away, *second_2), near_rows
    )
    second_3 = step(all_after(second_2, away))
    second_4 = last_step(all_after(second_3, kept))
    kept_near = exchanged(kept, "blk")
    pieces, rest = [columns, *both_1, *second_2, *second_3], quarter - first
    far_sums, own_sums, far_cut, own_cut = most(
        pieces, first, rest, far_rows, far_near_rows, own_rows, near_rows
    )
    away = last_projected(ids, positions, second_4, far_sums, far_cut, 0)
    last_back = exchanged(away, "groups")
    rest_kept = last_projected(
        ids, positions, second_4, after(own_sums, away), own_cut, 22_000_000_000
    )
    back = after(back, *second_4)
    result = finish(
        [kept, kept_near, back, exchanged(back, "blk")],
        ((0, 0, 0, 0), (0, 1, tokens, 0), (1, 0, 0, 0), (1, 1, tokens, 0)),
        None,
    )
    result = finish(
        [rest_kept, exchanged(rest_kept, "blk")],
        ((0, 0, 0, first), (0, 1, tokens, first)),
        result,
    )
    last_back = after(last_back, result)
    last_near = exchanged(last_back, "blk")
    result = finish([last_back], ((1, 0, 0, first),), result)
    return finish([last_near], ((1, 1, tokens, first),), result)


def solution(mesh):
    in_specs = (
        P(("groups", "fsdp", "blk"), None),
        P("groups"),
        P(("groups", "fsdp", "blk"), None),
        P(("groups", "fsdp", "blk"), None, None),
        P(("groups", "fsdp", "blk"), None, None),
        P(("groups", "fsdp"), None, None),
        P(("groups", "fsdp"), None),
        P(("groups", "fsdp"), None, None),
        P("fsdp", None),
    )
    out_specs = P(("groups", "fsdp", "blk"), None)
    return jax.shard_map(local, mesh=mesh, in_specs=in_specs, out_specs=out_specs, check_vma=False)
```
